32 devices in a mesh: feat: 8 (over y, x, core), grp: 4 (over z).
Axes of the slice: x: 2, y: 2, z: 4, core: 2. Of those that a mesh axis runs over, the one named last changes fastest.
Arguments:
- node_features: bfloat16 [2048, 32768], P('feat', 'grp'), may hold values from -6 to 6
- neighbours: int32 [64, 16, 512], P('grp'), may hold values from 0 to 511, as said below
- edge_counts: int32 [64, 512], P('grp'), may hold values from 0 to 16, as said below
- first_weight_matrix: bfloat16 [2048, 2048], P(('feat', 'grp')), may hold values from -0.25 to 0.25
- bias_one: bfloat16 [2048], P(('feat', 'grp')), may hold values from -3 to 3
- weight_two: bfloat16 [2048, 2048], P(('feat', 'grp')), may hold values from -0.25 to 0.25
- bias_two: bfloat16 [2048], P(('feat', 'grp')), may hold values from -3 to 3
- cotangent: bfloat16 [2048, 32768], P(None, ('grp', 'feat')), may hold values from -6 to 6
Outputs:
- layer_output: bfloat16 [2048, 32768], P(None, ('grp', 'feat'))
- input_grad: float32 [2048, 32768], P('feat', 'grp')
- grad_weight_one: float32 [2048, 2048], P(('feat', 'grp'))
- grad_bias_one: float32 [2048], P(('feat', 'grp'))
- grad_weight_two: float32 [2048, 2048], P(('feat', 'grp'))
- grad_bias_two: float32 [2048], P(('feat', 'grp'))
The draws below stay inside these ranges and needn't reach their ends.
Inputs may be any that keep to these rules, and one draw needn't show every extreme that they name: `edge_counts`: in each cluster the nodes with edges are a prefix of its 512 slots, at least half of them, and one cluster of every draw uses all slots; such a node has 1 to 16 edges, one node of each cluster exactly 16; slots after the prefix have 0. `neighbours`: every entry names a slot inside its cluster's prefix of nodes with edges; entries at k >= edge_counts are not edges.
All inputs are finite; a program needn't handle non-finite values.
Results may differ from the reference program's by a relative error of at most 0.01.
Values may be sent and summed in bfloat16 or wider, within the bound.
A program may use at most 256 MiB of HBM per device.

```python
import jax
import jax.numpy as jnp
from jax import lax

F = 2048
CAP = 512
KMAX = 16
CLUSTERS = 64
NODES = 32768


def occupied_counts(key):
    drawn = jax.random.randint(jax.random.fold_in(key, 11), (CLUSTERS,), CAP // 2, CAP + 1)
    full_index = jax.random.randint(jax.random.fold_in(key, 12), (), 0, CLUSTERS)
    cluster_ids = jnp.arange(CLUSTERS, dtype=jnp.int32)
    return (jnp.where(cluster_ids == full_index, CAP, drawn).astype(jnp.int32), full_index)


def draw_edge_counts(key, part):
    sizes_live, full_index = occupied_counts(key)
    key = jax.random.fold_in(key, 3)
    edge_total = jax.random.randint(key, (CLUSTERS, CAP), 1, KMAX + 1)
    peak_row = jax.random.randint(jax.random.fold_in(key, 1), (CLUSTERS,), 0, CAP) % sizes_live
    row_ids = jnp.arange(CAP, dtype=jnp.int32)
    edge_total = jnp.where(row_ids[None, :] == peak_row[:, None], KMAX, edge_total)
    edge_total = jnp.where(row_ids[None, :] < sizes_live[:, None], edge_total, 0)
    return edge_total.astype(jnp.int32)


def draw_neighbours(key, part):
    sizes_live, full_index = occupied_counts(key)
    key = jax.random.fold_in(key, 5)
    raw_bits = jax.random.randint(key, (CLUSTERS, KMAX, CAP), 0, 2 ** 30)
    targets = raw_bits % sizes_live[:, None, None]
    cluster_ids = jnp.arange(CLUSTERS, dtype=jnp.int32)
    column_ids = jnp.arange(KMAX, dtype=jnp.int32)
    row_ids = jnp.arange(CAP, dtype=jnp.int32)
    marked = (cluster_ids[:, None, None] == full_index) & (column_ids[None, :, None] == 0) & (row_ids[None, None, :] == 0)
    return jnp.where(marked, CAP - 1, targets).astype(jnp.int32)


def shard_levels(key, dims, pieces, least, high):
    factor_of = 1.0
    for dim, blocks in pieces:
        steps = jax.random.uniform(jax.random.fold_in(jax.random.fold_in(key, 6), dim), (blocks,), jnp.float32, least / len(pieces), high / len(pieces))
        factor_of = factor_of * jnp.repeat(jnp.exp(steps), dims[dim] // blocks).reshape((-1,) + (1,) * (len(dims) - 1 - dim))
    return factor_of


def centred(key, dims, width, reach, shards=(), kind=jnp.bfloat16):
    gain = shard_levels(key, dims, shards, -0.22, 0.18) if shards else 1.0
    entries = jax.random.normal(key, dims, jnp.float32) * width * gain
    return jnp.minimum(jnp.maximum(entries, -reach), reach).astype(kind)


def setup_inputs(seed: int = 0) -> dict:
    arg_keys = jax.random.split(jax.random.key(seed), 9)
    node_features = centred(arg_keys[0], (F, NODES), 1.0, 6.0, ((0, 8), (1, 4)))
    neighbours = draw_neighbours(jax.random.fold_in(arg_keys[8], 71), 0)
    edge_counts = draw_edge_counts(jax.random.fold_in(arg_keys[8], 71), 0)
    first_weight_matrix = centred(arg_keys[3], (F, F), (F // 4) ** -0.5, 0.25, ((0, 32),))
    bias_one = centred(arg_keys[4], (F,), 0.5, 3.0, ((0, 32),))
    weight_two = centred(arg_keys[5], (F, F), (F // 4) ** -0.5, 0.25, ((0, 32),))
    bias_two = centred(arg_keys[6], (F,), 0.5, 3.0, ((0, 32),))
    cotangent = centred(arg_keys[7], (F, NODES), 1.0, 6.0, ((1, 32),))
    return {"node_features": node_features, "neighbours": neighbours, "edge_counts": edge_counts, "first_weight_matrix": first_weight_matrix, "bias_one": bias_one, "weight_two": weight_two, "bias_two": bias_two, "cotangent": cotangent}


PRECISE = lax.Precision.HIGHEST

@jax.custom_vjp
def low(v):
    return lax.optimization_barrier(v.astype(jnp.bfloat16)).astype(jnp.float32)

@jax.custom_vjp
def low_back(v):
    return v

def low_keep(v):
    return (low(v), None)

def low_pass(kept, grad):
    return (grad,)

def back_keep(v):
    return (v, None)

def back_low(kept, grad):
    return (low(grad),)
low.defvjp(low_keep, low_pass)
low_back.defvjp(back_keep, back_low)

def activate(value):
    return jax.nn.gelu(value, approximate=True)

def count_matrix(neighbours, edge_counts):
    positions = jnp.arange(CAP, dtype=jnp.int32)
    columns = jnp.arange(KMAX, dtype=jnp.int32)

    def cluster_block(cluster_item):
        targets, totals = cluster_item
        usable = columns[:, None] < totals[None, :]
        equality_mask = (targets[:, :, None] == positions[None, None, :]) & usable[:, :, None]
        return lax.optimization_barrier(jnp.sum(equality_mask.astype(jnp.float32), axis=0))
    return lax.map(cluster_block, (neighbours, edge_counts))

def reference(node_features, neighbours, edge_counts, first_weight_matrix, bias_one, weight_two, bias_two, cotangent):
    tile_operator = count_matrix(neighbours, edge_counts)
    totals = edge_counts.astype(jnp.float32)
    scaling = jnp.where(edge_counts > 0, 1.0 / (totals + 1.0), jnp.zeros_like(totals))

    def aggregate(field):
        cluster_blocks_padded = field.reshape(CLUSTERS, CAP, F)
        summed_rows = jnp.einsum('cij,cjd->cid', tile_operator, cluster_blocks_padded, precision=PRECISE) + 2.0 * cluster_blocks_padded
        summed_rows = low_back(summed_rows)
        return (scaling[:, :, None] * summed_rows).reshape(NODES, F)

    def forward_pass(features, w_one, b_one, w_two, b_two):
        rows_one = low(low_back(aggregate(features)))
        pre_one = low_back(jnp.dot(rows_one, w_one, precision=PRECISE) + b_one)
        hidden = low(low_back(activate(pre_one)))
        rows_two = low(low_back(aggregate(hidden)))
        pre_two = low_back(jnp.dot(rows_two, w_two, precision=PRECISE) + b_two)
        return activate(pre_two)
    final_result, pullback = jax.vjp(forward_pass, node_features.astype(jnp.float32).T, first_weight_matrix.astype(jnp.float32), bias_one.astype(jnp.float32), weight_two.astype(jnp.float32), bias_two.astype(jnp.float32))
    grad_input, grad_w_one, grad_b_one, grad_w_two, grad_b_two = pullback(cotangent.astype(jnp.float32).T)
    return (final_result.T.astype(jnp.bfloat16), grad_input.T, grad_w_one, grad_b_one, grad_w_two, grad_b_two)
```

```python
import jax
import jax.numpy as jnp
from jax import lax
from jax.sharding import PartitionSpec as P


def activate(value):
    return jax.nn.gelu(value, approximate=True)


def body(features, neighbours, edge_counts, w_one, b_one, w_two, b_two, cotangent):
    nf = lax.axis_size("feat")
    capacity = edge_counts.shape[1]
    own = edge_counts.shape[0] // nf
    first = lax.axis_index("feat") * own
    near = lax.dynamic_slice_in_dim(neighbours, first, own, 0)
    totals = lax.dynamic_slice_in_dim(edge_counts, first, own, 0)
    steps = jnp.arange(near.shape[1], dtype=jnp.int32)
    near = jnp.where(steps[None, :, None] < totals[:, None, :], near, -1)
    slots = jnp.arange(capacity, dtype=jnp.int32)
    counts_t = jnp.sum(
        (near[:, :, None, :] == slots[None, None, :, None]).astype(jnp.float32), axis=1
    ).astype(jnp.bfloat16)
    live = totals.astype(jnp.float32)
    scaling = jnp.where(totals > 0, 1.0 / (live + 1.0), 0.0)

    w_one, w_two, b_one, b_two = (
        lax.all_gather(v, ("feat", "grp"), axis=0, tiled=True) for v in (w_one, w_two, b_one, b_two)
    )

    def aggregate(field):
        blocks = field.reshape(field.shape[0], own, capacity)
        summed = jnp.einsum("fuj,uji->fui", blocks, counts_t, preferred_element_type=jnp.float32)
        summed = summed + 2.0 * blocks.astype(jnp.float32)
        return (scaling[None] * summed).reshape(field.shape).astype(jnp.bfloat16)

    def aggregate_back(grad):
        blocks = grad.reshape(grad.shape[0], own, capacity).astype(jnp.float32)
        normed = (scaling[None] * blocks).astype(jnp.bfloat16)
        summed = jnp.einsum("fui,uji->fuj", normed, counts_t, preferred_element_type=jnp.float32)
        return (summed + 2.0 * normed.astype(jnp.float32)).reshape(grad.shape).astype(jnp.bfloat16)

    def linear(rows, weight, bias):
        product = lax.dot_general(
            weight, rows, (((0,), (0,)), ((), ())), preferred_element_type=jnp.float32
        )
        return product + bias.astype(jnp.float32)[:, None]

    def weight_term(rows, grad_pre):
        term = lax.dot_general(
            rows, grad_pre, (((1,), (1,)), ((), ())), preferred_element_type=jnp.float32
        )
        return lax.psum_scatter(
            term.astype(jnp.bfloat16), ("feat", "grp"), scatter_dimension=0, tiled=True
        ).astype(jnp.float32)

    def bias_term(grad_pre):
        return lax.psum_scatter(
            jnp.sum(grad_pre.astype(jnp.float32), axis=1),
            ("feat", "grp"),
            scatter_dimension=0,
            tiled=True,
        )

    field = lax.all_to_all(features, "feat", split_axis=1, concat_axis=0, tiled=True)
    rows_one = aggregate(field)
    pre_one = linear(rows_one, w_one, b_one)
    hidden, back_one = jax.vjp(activate, pre_one)
    rows_two = aggregate(hidden.astype(jnp.bfloat16))
    pre_two = linear(rows_two, w_two, b_two)
    output, back_two = jax.vjp(activate, pre_two)
    grad_pre_two = back_two(cotangent.astype(jnp.float32))[0].astype(jnp.bfloat16)
    grad_w_two = weight_term(rows_two, grad_pre_two)
    grad_rows_two = jnp.dot(w_two, grad_pre_two, preferred_element_type=jnp.float32)
    grad_hidden = aggregate_back(grad_rows_two.astype(jnp.bfloat16))
    grad_pre_one = back_one(grad_hidden.astype(jnp.float32))[0].astype(jnp.bfloat16)
    grad_w_one = weight_term(rows_one, grad_pre_one)
    grad_rows_one = jnp.dot(w_one, grad_pre_one, preferred_element_type=jnp.float32)
    grad_field = aggregate_back(grad_rows_one.astype(jnp.bfloat16))
    input_grad = lax.all_to_all(grad_field, "feat", split_axis=0, concat_axis=1, tiled=True)
    return (
        output.astype(jnp.bfloat16),
        input_grad.astype(jnp.float32),
        grad_w_one,
        bias_term(grad_pre_one),
        grad_w_two,
        bias_term(grad_pre_two),
    )


def solution(mesh):
    both = ("feat", "grp")
    in_specs = (
        P("feat", "grp"),
        P("grp", None, None),
        P("grp", None),
        P(both, None),
        P(both),
        P(both, None),
        P(both),
        P(None, ("grp", "feat")),
    )
    out_specs = (
        P(None, ("grp", "feat")),
        P("feat", "grp"),
        P(both, None),
        P(both),
        P(both, None),
        P(both),
    )
    return jax.shard_map(body, mesh=mesh, in_specs=in_specs, out_specs=out_specs, check_vma=False)
```

```python
import functools

import jax
import jax.numpy as jnp
from jax import lax
from jax.experimental import pallas as pl
from jax.experimental.pallas import tpu as pltpu
from jax.sharding import PartitionSpec as P

BF, F32 = jnp.bfloat16, jnp.float32
MESH = pl.DeviceIdType.MESH
TILES = 4
NN = (((1,), (0,)), ((), ()))
NT = (((1,), (1,)), ((), ()))
TN = (((0,), (0,)), ((), ()))
GATHER_ONE = ("yxz", "yxz", "zxy", "zyx")
GATHER_TWO = ("yxz", "xyz", "zxy", "zyx")
REDUCE_TWO = ("xyz", "yxz", "yxz", "zyx")
REDUCE_ONE = ("zxy", "zyx", "yxz", "xyz")
ORDER = (
    ("g1", 2), ("g1", 0), ("xs", 2), ("g2", 3), ("g2", 1), ("g1", 0), ("gb", 0), ("g1", 3), ("g1", 2),
    ("g2", 1), ("g2", 2), ("gb", 0), ("xs", 5), ("g1", 1), ("xs", 1), ("xs", 6), ("g1", 0), ("cnt", 0),
    ("g2", 2), ("g1", 3), ("cnt", 1), ("gb", 0), ("g2", 0), ("cnt", 2), ("g1", 1), ("g2", 1), ("cnt", 3),
    ("g1", 3), ("g2", 3), ("xa", 1), ("g1", 2), ("xs", 0), ("g1", 0), ("xs", 4), ("xs", 3), ("xa", 2),
    ("g2", 0), ("g1", 0), ("g2", 1), ("g1", 2), ("gb", 0), ("xa", 7), ("gb", 0), ("g1", 3), ("g1", 0),
    ("g2", 3), ("xa", 0), ("g1", 1), ("g2", 0), ("g2", 2), ("gb", 0), ("xa", 3), ("g1", 2), ("xa", 4),
    ("xa", 5), ("g1", 1), ("g1", 3), ("xa", 6), ("g2", 3), ("g1", 2), ("l1", 2), ("g1", 3), ("g2", 2),
    ("g2", 0), ("g1", 1), ("g2", 1), ("l1", 3), ("l1", 0), ("g2", 0), ("g2", 3), ("g2", 1), ("g1", 1),
    ("l1", 1), ("g2", 0), ("g2", 2), ("l2", 0), ("g2", 3), ("l2", 1), ("g2", 2), ("l2", 2), ("l2", 3),
    ("s2", 2), ("s2", 0), ("s2", 1), ("o2", 2), ("r2", 2), ("s2", 3), ("o2", 0), ("o2", 1), ("r2", 0),
    ("r2", 1), ("o2", 3), ("r2", 3), ("b2", 3), ("b2", 0), ("b2", 2), ("r2", 2), ("r2", 3), ("b2", 1),
    ("b1", 0), ("s1", 2), ("r2", 2), ("s1", 3), ("s1", 1), ("r2", 2), ("r2", 0), ("o1", 2), ("o1", 3),
    ("o1", 1), ("r1", 1), ("r2", 2), ("s1", 0), ("o1", 0), ("r2", 1), ("r1", 3), ("r2", 0), ("r1", 2),
    ("b1", 1), ("r2", 3), ("r2", 1), ("r1", 1), ("bs", 0), ("rb", 0), ("r1", 1), ("r1", 3), ("r1", 0),
    ("r1", 2), ("b1", 2), ("r2", 1), ("r2", 1), ("r2", 0), ("r1", 3), ("r1", 0), ("r2", 3), ("rb", 0),
    ("r2", 0), ("r1", 0), ("r1", 1), ("rb", 0), ("r1", 2), ("r1", 3), ("r1", 0), ("r1", 2), ("b1", 3),
    ("rb", 0), ("r1", 3), ("r1", 1), ("r1", 0), ("r1", 2), ("r2", 3), ("rb", 0),
)


def dot(a, b, dims):
    return lax.dot_general(a, b, dims, preferred_element_type=F32)


def gelu_and_slope(v):
    c = 0.7978845608
    square = v * v
    half = 0.5 + 0.5 * jnp.tanh(v * (c + (c * 0.044715) * square))
    value = v * half
    slope = half + (value - value * half) * (2.0 * c + (6.0 * c * 0.044715) * square)
    return value, slope


def kernel(
    sizes,
    x_in, near_in, edges_in, w_one_in, w_two_in, b_one_in, b_two_in, cot_in,
    out_ref, grad_in_ref, grad_one_ref, grad_two_ref, grad_bias_ref,
    w_one, w_two, rows_one, rows_two, slope_one, grad_two, terms, pair, got_one, got_two, relays,
    counts, scaling, near, biases, bias_sum, bias_terms, bias_pair, bias_got, bias_relay,
    send, recv, local, credit,
):
    Y, X, Z, r, width, cap, own = sizes
    planes, nf = Y * X, 2 * Y * X
    per = planes // TILES
    slots = own * cap
    cols_per = width // TILES
    rows_per = width // TILES
    f, z = lax.axis_index("feat"), lax.axis_index("grp")
    c = lax.rem(f, 2)
    x = lax.rem(lax.div(f, 2), X)
    y = lax.div(f, 2 * X)
    place = {"y": y, "x": x, "c": c, "z": z}
    extent = {"y": Y, "x": X, "z": Z}
    taken = [0, 0]
    pending = []
    pending_two = []

    def device(**moved):
        at = {**place, **moved}
        return ((at["y"] * X + at["x"]) * 2 + at["c"], at["z"])

    def copy_to(src, dst, dev, arrival=None):
        taken[0] += 1
        if arrival is None:
            taken[1] += 1
            arrival = taken[1] - 1
        return pltpu.make_async_remote_copy(
            src, dst, send.at[taken[0] - 1], recv.at[arrival], device_id=dev, device_id_type=MESH
        )

    def launch(copy, when=None, log=pending):
        if when is None:
            copy.start()
        else:
            pl.when(when)(copy.start)
        log.append((copy, when))

    def settle(copies):
        for copy, when in copies:
            if when is None:
                copy.wait_send()
            else:
                pl.when(when)(copy.wait_send)

    def arrived(copy, when=None):
        if when is None:
            copy.wait_recv()
        else:
            pl.when(when)(copy.wait_recv)

    def box(ref, cols, full, **moved):
        at = {**place, **moved}
        lead = [slice(None) if a in full else pl.ds(at[a], 1) for a in ("y", "x", "c", "z")]
        return ref.at[(*lead, slice(None), cols)]

    ends = jnp.logical_or(z == 0, z == Z - 1)
    inner = jnp.logical_not(ends)

    def flip(coordinate, bit):
        return coordinate + bit - 2 * bit * lax.rem(lax.div(coordinate, bit), 2)

    def around(axis, hop):
        return lax.rem(place[axis] + hop, extent[axis])

    def gather(ref, cols, first, order, log=pending):
        full = set()
        for stage, axis in enumerate(order):
            src = box(ref, cols, full)
            if stage == 0 and first is not None:
                src = first.at[(slice(None),) * 5 + (cols,)]
            copies = []
            if axis == "z":
                far = flip(z, 2)
                to_far = copy_to(src, box(ref, cols, full), device(z=far))
                to_near = copy_to(src, box(ref, cols, full), device(z=flip(z, 1)))
                to_end = copy_to(src, box(ref, cols, full), device(z=Z - 1 - z))
                handed = taken[1] - 1
                launch(to_far, None, log)
                launch(to_near, None, log)
                launch(to_end, inner, log)
                yield
                arrived(to_far)
                moved = box(ref, cols, full, z=far)
                launch(copy_to(moved, moved, device(z=flip(z, 1)), handed), inner, log)
                yield
                arrived(to_near)
                arrived(to_end)
            else:
                for hop in range(1, extent[axis]):
                    dev = device(**{axis: around(axis, hop)})
                    copies.append(copy_to(src, box(ref, cols, full), dev))
                    launch(copies[-1], None, log)
                yield
                for copy in copies:
                    arrived(copy)
            full.add(axis)
        whole = box(ref, cols, full)
        copy = copy_to(whole, whole, device(c=1 - c))
        launch(copy, None, log)
        yield
        arrived(copy)

    def reduce(ref, got, cols, order, result, relay):
        full = {"x", "y", "z"}

        def total(boxes, extra=None):
            value = box(ref, cols, full)[...].astype(F32)
            for part in boxes:
                value = value + part[...].astype(F32)
            return value

        def here(target, **moved):
            at = {"y": y, "x": x, "c": 0 * c, "z": z, **moved}
            lead = [slice(None) if a in full else pl.ds(at[a], 1) for a in ("y", "x", "c", "z")]
            return target.at[(*lead, slice(None), cols)]

        for stage, axis in enumerate(order):
            last = stage == len(order) - 1
            full.discard(axis)
            parts = []
            if axis == "z":
                near_z, far_z, end_z = flip(z, 1), flip(z, 2), Z - 1 - z
                to_near = copy_to(box(ref, cols, full, z=near_z), here(got), device(z=near_z))
                to_far = copy_to(box(ref, cols, full, z=far_z), here(got), device(z=far_z))
                to_end = copy_to(box(ref, cols, full, z=end_z), here(got), device(z=end_z))
                lead = [slice(None) if a in full else pl.ds(place[a], 1) for a in ("y", "x")]
                handed = here(got, z=near_z)
                held = here(got)
                if not last:
                    handed = held = relay.at[(*lead, slice(None), slice(None), slice(None), slice(None))]
                via = copy_to(box(ref, cols, full, z=end_z), handed, device(z=near_z))
                launch(via, ends)
                launch(to_far, ends)
                launch(to_near)
                launch(to_end, inner)
                yield
                arrived(via, inner)

                @pl.when(inner)
                def _():
                    mine = box(ref, cols, full, z=far_z)
                    mine[...] = (mine[...].astype(F32) + held[...].astype(F32)).astype(mine.dtype)

                launch(to_far, inner)
                yield
                arrived(to_near)
                arrived(to_far)
                arrived(to_end, inner)
                value = total([here(got, z=near_z), here(got, z=far_z)])
                if last:
                    result(value, cols)

                    @pl.when(inner)
                    def _():
                        result(here(got, z=end_z)[...].astype(F32), cols, True)
                else:
                    mine = box(ref, cols, full)
                    more = here(got, z=end_z)[...].astype(F32)
                    mine[...] = (value + jnp.where(inner, more, 0.0)).astype(mine.dtype)
            else:
                for hop in range(1, extent[axis]):
                    target = around(axis, hop)
                    copy = copy_to(
                        box(ref, cols, full, **{axis: target}), here(got), device(**{axis: target})
                    )
                    launch(copy)
                    parts.append((copy, here(got, **{axis: around(axis, extent[axis] - hop)})))
                yield
                for copy, _ in parts:
                    arrived(copy)
                value = total([part for _, part in parts])
                if last:
                    result(value, cols)
                else:
                    mine = box(ref, cols, full)
                    mine[...] = value.astype(mine.dtype)

    def finish(*parts):
        for part in parts:
            for _ in part:
                pass

    def rows_of(w, q):
        if per < X:
            lead = (pl.ds(lax.div(q * per, X), 1), pl.ds(lax.rem(q * per, X), per))
        else:
            lead = (pl.ds(q * (per // X), per // X), slice(None))
        return w.at[(*lead, slice(None), slice(None), slice(None), slice(None))]

    def act_rows(ref, q):
        return ref.at[pl.ds(q * per, per)]

    def tile_cols(u):
        return pl.ds(pl.multiple_of(u * cap, cap), cap)

    def each_cluster(work):
        def one(u, carry):
            work(u)
            return carry

        lax.fori_loop(0, own, one, 0)

    barrier = pltpu.get_barrier_semaphore()
    for hop in range(1, nf):
        pl.semaphore_signal(barrier, 1, device_id=(lax.rem(f + hop, nf), z), device_id_type=MESH)
    for hop in range(1, Z):
        pl.semaphore_signal(barrier, 1, device_id=(f, lax.rem(z + hop, Z)), device_id_type=MESH)

    every = slice(0, 128)
    parts = [slice(q * cols_per, (q + 1) * cols_per) for q in range(TILES)]
    near_copy = pltpu.make_async_copy(near_in.at[pl.ds(f * own, own)], near, local.at[0])
    w_one_copy = pltpu.make_async_copy(w_one_in, box(w_one, slice(None), ()), local.at[1])
    w_two_copy = pltpu.make_async_copy(w_two_in, box(w_two, slice(None), ()), local.at[2])
    x_copy = pltpu.make_async_copy(
        x_in.at[:, pl.ds(pl.multiple_of(f * slots, slots), slots)],
        rows_one.at[lax.div(f, 2), c],
        local.at[3],
    )
    cot_copy = pltpu.make_async_copy(cot_in, grad_two, local.at[4])
    near_copy.start()
    w_one_copy.start()
    w_two_copy.start()
    x_copy.start()
    shape = (r, r)
    same = lax.broadcasted_iota(jnp.int32, shape, 0) == lax.broadcasted_iota(jnp.int32, shape, 1)
    lane = lax.broadcasted_iota(jnp.int32, (r, 128), 1)
    block = jnp.zeros((r, 128), F32)
    for layer, ref in enumerate((b_one_in, b_two_in)):
        column = jnp.sum(jnp.where(same, ref[...].astype(F32), 0.0), axis=1, keepdims=True)
        block = jnp.where(lane == layer, column, block)
    box(biases, every, ())[...] = block.astype(BF).reshape(1, 1, 1, 1, r, 128)

    pl.semaphore_wait(barrier, nf - 1 + Z - 1)

    work = {}
    for q, cols in enumerate(parts):
        work["g1", q] = gather(w_one, cols, w_one_in, GATHER_ONE[q])
        work["g2", q] = gather(w_two, cols, w_two_in, GATHER_TWO[q], pending_two)
    work["gb", 0] = gather(biases, every, None, "xyz")

    turns = [(dy, dx, dc) for dc in range(2) for dy in range(Y) for dx in range(X)][1:]
    turns.sort(key=lambda turn: (turn[0] > 0) + (turn[1] > 0))
    groups = [turns[i * len(turns) // 7 : (i + 1) * len(turns) // 7] for i in range(7)]
    x_copies = {}

    def send_x(i):
        for dy, dx, dc in groups[i]:
            dev = device(y=lax.rem(y + dy, Y), x=lax.rem(x + dx, X), c=lax.rem(c + dc, 2))
            mine = x_in.at[:, pl.ds(pl.multiple_of(dev[0] * slots, slots), slots)]
            x_copies[dy, dx, dc] = copy_to(mine, rows_one.at[lax.div(f, 2), c], dev)
            launch(x_copies[dy, dx, dc])

    strip = min(64, cap)
    strips = cap // strip

    def count(i):
        u, part = i * own // 4, i % (4 // own)
        if i == 0:
            near_copy.wait()
            bias_sum[...] = jnp.zeros_like(bias_sum)
        edges = edges_in[pl.ds(f * own + u, 1), :]
        total_edges = edges.astype(F32)
        near_u = near.at[u]
        scaling[u] = jnp.where(edges > 0, 1.0 / (total_edges + 1.0), 0.0)

        def strip_counts(i, carry):
            start = pl.multiple_of(i * strip, strip)
            slot = start + lax.broadcasted_iota(jnp.int32, (strip, cap), 0)
            other = lax.broadcasted_iota(jnp.int32, (strip, cap), 1)
            acc = jnp.where(slot == other, 2.0, 0.0)
            for k in range(near.shape[1]):
                target = jnp.where(k < edges, near_u[k : k + 1, :], -1)
                acc = acc + jnp.where(slot == target, 1.0, 0.0)
            counts[u, pl.ds(start, strip), :] = acc.astype(BF)
            return carry

        share = strips * own // 4
        lax.fori_loop(part * share, (part + 1) * share, strip_counts, 0)

    def aggregate(value, u):
        return (scaling[u] * dot(value, counts[u], NN)).astype(BF)

    def aggregate_back(value, u):
        normed = (scaling[u] * value.astype(BF).astype(F32)).astype(BF)
        return dot(normed, counts[u], NT)

    def first_rows(owner):
        ref = rows_one.at[lax.div(owner, 2), lax.rem(owner, 2)]

        def work(u):
            ref[:, tile_cols(u)] = aggregate(ref[:, tile_cols(u)], u)

        each_cluster(work)

    def rows_from(i):
        if i == 7:
            x_copy.wait()
            first_rows(f)
            return
        for dy, dx, dc in groups[i]:
            arrived(x_copies[dy, dx, dc])
            owner = device(
                y=lax.rem(y + Y - dy, Y), x=lax.rem(x + X - dx, X), c=lax.rem(c + dc, 2)
            )
            first_rows(owner[0])

    def linear(w, rows, layer, q, u):
        weight = w[..., parts[q]].reshape(width, cols_per)
        a = rows[:, :, :, tile_cols(u)].reshape(width, cap)
        bias = rows_of(biases, q)[...].reshape(rows_per, 128)[:, layer : layer + 1]
        return dot(weight, a, TN) + bias.astype(F32)

    tile = (per, 2, Z * r, cap)

    def layer_one(q):
        def work(u):
            value, slope = gelu_and_slope(linear(w_one, rows_one, 0, q, u))
            act_rows(slope_one, q)[:, :, :, tile_cols(u)] = slope.astype(BF).reshape(tile)
            rows = aggregate(value.astype(BF), u)
            act_rows(rows_two, q)[:, :, :, tile_cols(u)] = rows.reshape(tile)

        each_cluster(work)

    def add_bias(q, u, value):
        ref = bias_sum.at[pl.ds(q * rows_per, rows_per), :]
        folded = sum(value[:, i * 128 : (i + 1) * 128] for i in range(cap // 128))
        ref[...] = ref[...] + folded

    out_copies = []

    def layer_two(q):
        if not out_copies:
            cot_copy.wait()

        def work(u):
            value, slope = gelu_and_slope(linear(w_two, rows_two, 1, q, u))
            ref = rows_of(terms, q).at[..., tile_cols(u)]
            ref[...] = value.astype(BF).reshape(ref.shape)
            ref = act_rows(grad_two, q).at[:, :, :, tile_cols(u)]
            grad = (ref[...].astype(F32).reshape(rows_per, cap) * slope).astype(BF)
            ref[...] = grad.reshape(tile)
            add_bias(q, u, grad.astype(F32))

        each_cluster(work)

        copy = pltpu.make_async_copy(
            rows_of(terms, q).at[..., pl.ds(0, slots)], rows_of(out_ref, q), local.at[5 + q]
        )
        copy.start()
        out_copies.append(copy)

    lanes = lax.broadcasted_iota(jnp.int32, (width, 128), 1)

    def bias_of_two():
        total = jnp.where(lanes == 1, jnp.sum(bias_sum[...], axis=1, keepdims=True), 0.0)
        bias_terms[...] = total.astype(BF).reshape(bias_terms.shape)
        bias_sum[...] = jnp.zeros_like(bias_sum)

    def pair_half(rows, grads, core, q):
        a = rows[:, pl.ds(core, 1)].reshape(width // 2, slots)
        b = act_rows(grads, q)[...].reshape(rows_per, slots)
        return dot(a, b, NT).reshape(Y, X, 1, Z, r, cols_per)

    def pair_send(target, q, value):
        half = target.at[:, :, pl.ds(1 - c, 1), :, :, parts[q]]
        half[...] = value.astype(BF)
        copy = copy_to(half, pair.at[..., parts[q]], device(c=1 - c))
        launch(copy)
        return copy

    def pair_add(target, q, value, copy):
        arrived(copy)
        half = target.at[:, :, pl.ds(c, 1), :, :, parts[q]]
        half[...] = (value + pair[..., parts[q]].astype(F32)).astype(BF)

    def owner_result(ref):
        def result(value, cols, add=False):
            value = value.reshape(r, value.shape[-1])
            ref[:, cols] = ref[:, cols] + value if add else value

        return result

    layers = {
        "1": (rows_one, rows_two, w_two, got_one, REDUCE_ONE, grad_one_ref),
        "2": (rows_two, grad_two, terms, got_two, REDUCE_TWO, grad_two_ref),
    }
    relayed = 0
    for name, (_, _, target, got, orders, out) in layers.items():
        for q in range(TILES):
            relay = None
            if orders[q][0] == "z":
                relay = relays.at[..., relayed * cols_per : (relayed + 1) * cols_per]
                relayed += 1
            work["r" + name, q] = reduce(target, got, parts[q], orders[q], owner_result(out), relay)
    work["rb", 0] = reduce(
        bias_terms, bias_got, every, "zyx", owner_result(grad_bias_ref), bias_relay
    )
    pair_copies = {}
    seen = set()

    def once(name):
        first = name not in seen
        seen.add(name)
        return first

    def sibling_half(name, q):
        if name == "2":
            if q * cols_per < slots and once("out"):
                for copy in out_copies:
                    copy.wait()
        elif once("s1"):
            settle(pending_two)
            pl.semaphore_wait(credit, 1)
        rows, grads, target = layers[name][:3]
        pair_copies[name, q] = pair_send(target, q, pair_half(rows, grads, 1 - c, q))

    def own_half(name, q):
        rows, grads, target = layers[name][:3]
        pair_add(target, q, pair_half(rows, grads, c, q), pair_copies[name, q])
        if name == "2":
            seen.add(("pair", q))
            if all(("pair", i) in seen for i in range(TILES)):
                pl.semaphore_signal(credit, 1, device_id=device(c=1 - c), device_id_type=MESH)

    def back_two(q):
        if once("b2"):
            bias_of_two()

        def work(u):
            weight = rows_of(w_two, q)[...].reshape(rows_per, width)
            grad = dot(weight, grad_two[:, :, :, tile_cols(u)].reshape(width, cap), NN)
            hidden = aggregate_back(grad, u).astype(BF).astype(F32)
            slope = act_rows(slope_one, q)[:, :, :, tile_cols(u)].reshape(rows_per, cap).astype(F32)
            grad = (hidden * slope).astype(BF)
            act_rows(rows_two, q)[:, :, :, tile_cols(u)] = grad.reshape(tile)
            add_bias(q, u, grad.astype(F32))

        each_cluster(work)

    grad_one = rows_two
    def bias_send():
        total = jnp.sum(bias_sum[...], axis=1, keepdims=True)
        both = jnp.where(lanes == 0, total, bias_terms[...].reshape(width, 128).astype(F32))
        bias_terms[...] = both.astype(BF).reshape(bias_terms.shape)
        copy = copy_to(bias_terms.at[:, :, pl.ds(1 - c, 1)], bias_pair, device(c=1 - c))
        launch(copy)
        pair_copies["b"] = copy

    def bias_add():
        arrived(pair_copies["b"])
        mine = bias_terms.at[:, :, pl.ds(c, 1)]
        mine[...] = (mine[...].astype(F32) + bias_pair[...].astype(F32)).astype(BF)

    grad_in = grad_two
    grad_place = grad_in_ref.at[:, pl.ds(pl.multiple_of(f * slots, slots), slots)]

    def back_one(i):
        k = (3, 1, 2, 0)[i]
        if per == 1:
            q = lax.rem(y + k // 2, Y) * X + lax.rem(x + k % 2, X)
        else:
            q = lax.rem(y + k, Y)

        def work(u):
            weight = rows_of(w_one, q)[...].reshape(rows_per, width)
            grad = dot(weight, grad_one[:, :, :, tile_cols(u)].reshape(width, cap), NN)
            value = aggregate_back(grad, u).astype(BF)
            act_rows(grad_in, q)[:, :, :, tile_cols(u)] = value.reshape(tile)

        each_cluster(work)
        for j in range(2 * per):
            to = q * (2 * per) + j
            hop = lax.rem(to + nf - f, nf)
            taken[0] += 1
            copy = pltpu.make_async_remote_copy(
                grad_in.at[lax.div(to, 2), lax.rem(to, 2)], grad_place,
                send.at[taken[0] - 1], recv.at[recv.shape[0] - nf + hop],
                device_id=(to, z), device_id_type=MESH,
            )
            launch(copy, None if k else to != f)

    calls = {
        "xs": send_x, "xa": rows_from, "cnt": count, "l1": layer_one, "l2": layer_two,
        "s1": functools.partial(sibling_half, "1"), "o1": functools.partial(own_half, "1"),
        "s2": functools.partial(sibling_half, "2"), "o2": functools.partial(own_half, "2"),
        "b2": back_two, "b1": back_one,
    }
    places = {}
    for name, q in ORDER:
        if name in calls:
            calls[name](q)
        elif name == "bs":
            bias_send()
        else:
            stage = places[name, q] = places.get((name, q), -1) + 1
            if stage == 0 and name == "rb":
                bias_add()
            if stage == 1 and name[0] == "g" and once("shards"):
                w_one_copy.wait()
                w_two_copy.wait()
                cot_copy.start()
            next(work[name, q], None)
            if stage == 5:
                finish(work[name, q])
    finish(*work.values())
    own_copy = pltpu.make_async_copy(grad_in.at[lax.div(f, 2), c], grad_place, local.at[0])
    own_copy.start()
    for hop in range(1, nf):
        sender = lax.rem(f + nf - hop, nf)
        pltpu.make_async_remote_copy(
            grad_in.at[0, 0], grad_in_ref.at[:, pl.ds(pl.multiple_of(sender * slots, slots), slots)],
            send.at[0], recv.at[recv.shape[0] - nf + hop],
            device_id=(f, z), device_id_type=MESH,
        ).wait_recv()
    own_copy.wait()
    settle(pending)


def body(mesh, features, neighbours, edge_counts, w_one, b_one, w_two, b_two, cotangent):
    nf, Z = mesh.shape["feat"], mesh.shape["grp"]
    side = 1
    while side * side * 2 < nf:
        side *= 2
    Y = X = side
    r, width = w_one.shape
    clusters, cap = edge_counts.shape
    own = clusters // nf
    slots = own * cap
    planes = Y * X
    group = features.shape[0]
    shard = (1, 1, 1, 1, r, width)
    act = (planes, 2, group, slots)
    table = (Y, X, 2, Z, r, width)
    half = (Y, X, 1, Z, r, width)
    anywhere = pl.BlockSpec(memory_space=pl.ANY)
    vmem = pl.BlockSpec(memory_space=pltpu.VMEM)
    scratch = [pltpu.VMEM(table, BF)] * 2
    scratch += [pltpu.VMEM(act, BF)] * 4
    scratch += [pltpu.VMEM(table, BF)] + [pltpu.VMEM(half, BF)] * 3
    relayed = sum(order[0] == "z" for order in REDUCE_ONE + REDUCE_TWO)
    scratch += [pltpu.VMEM((Y, X, 1, 1, r, max(1, relayed) * (width // TILES)), BF)]
    scratch += [
        pltpu.VMEM((own, cap, cap), BF),
        pltpu.VMEM((own, 1, cap), F32),
        pltpu.VMEM((own, *neighbours.shape[1:]), jnp.int32),
        pltpu.VMEM((Y, X, 2, Z, r, 128), BF),
        pltpu.VMEM((width, 128), F32),
        pltpu.VMEM((Y, X, 2, Z, r, 128), BF),
        pltpu.VMEM((Y, X, 1, Z, r, 128), BF),
        pltpu.VMEM((Y, X, 1, Z, r, 128), BF),
        pltpu.VMEM((Y, X, 1, 1, r, 128), BF),
        pltpu.SemaphoreType.DMA((256,)),
        pltpu.SemaphoreType.DMA((256,)),
        pltpu.SemaphoreType.DMA((16,)),
        pltpu.SemaphoreType.REGULAR,
    ]
    out, grad_in, grad_one, grad_two, grad_bias = pl.pallas_call(
        functools.partial(kernel, (Y, X, Z, r, width, cap, own)),
        out_shape=(
            jax.ShapeDtypeStruct((Y, X, 2, Z, r, slots), BF),
            jax.ShapeDtypeStruct((group, nf * slots), BF),
            jax.ShapeDtypeStruct((r, width), F32),
            jax.ShapeDtypeStruct((r, width), F32),
            jax.ShapeDtypeStruct((r, 128), F32),
        ),
        in_specs=[anywhere, anywhere, vmem, anywhere, anywhere, vmem, vmem, anywhere],
        out_specs=(anywhere, anywhere, vmem, vmem, vmem),
        scratch_shapes=scratch,
        compiler_params=pltpu.CompilerParams(
            collective_id=0, has_side_effects=True, vmem_limit_bytes=67_000_000
        ),
    )(
        features,
        neighbours,
        edge_counts,
        w_one.reshape(shard),
        w_two.reshape(shard),
        b_one.reshape(1, r),
        b_two.reshape(1, r),
        cotangent.reshape(act),
    )
    return (
        out.reshape(width, slots),
        grad_in.astype(F32),
        grad_one,
        grad_bias[:, 0],
        grad_two,
        grad_bias[:, 1],
    )


def solution(mesh):
    both = ("feat", "grp")
    in_specs = (
        P("feat", "grp"),
        P("grp", None, None),
        P("grp", None),
        P(both, None),
        P(both),
        P(both, None),
        P(both),
        P(None, ("grp", "feat")),
    )
    out_specs = (
        P(None, ("grp", "feat")),
        P("feat", "grp"),
        P(both, None),
        P(both),
        P(both, None),
        P(both),
    )
    return jax.shard_map(
        functools.partial(body, mesh), mesh=mesh, in_specs=in_specs, out_specs=out_specs, check_vma=False
    )
```

```python
import functools

import jax
import jax.numpy as jnp
from jax import lax
from jax.experimental import pallas as pl
from jax.experimental.pallas import tpu as pltpu
from jax.sharding import PartitionSpec as P

BF, F32 = jnp.bfloat16, jnp.float32
MESH = pl.DeviceIdType.MESH
TILES = 4
NN = (((1,), (0,)), ((), ()))
NT = (((1,), (1,)), ((), ()))
TN = (((0,), (0,)), ((), ()))
GATHER_ONE = ("xyz", "yxz", "xyz", "zyx")
GATHER_TWO = ("zyx", "yxz", "zyx", "zxy")
REDUCE_TWO = ("xyz", "yxz", "zxy", "zyx")
REDUCE_ONE = ("zxy", "yxz", "zxy", "yxz")
ORDER = (
    ("gb", 0), ("g1", 1), ("g1", 0), ("g1", 3), ("xs", 6), ("g2", 3), ("cnt", 0), ("g1", 0), ("gb", 0),
    ("g1", 1), ("cnt", 1), ("xs", 2), ("xs", 12), ("g1", 2), ("g2", 2), ("xs", 8), ("xs", 4), ("g1", 3),
    ("xs", 10), ("cnt", 2), ("gb", 0), ("g1", 0), ("xs", 7), ("xs", 9), ("xa", 14), ("g1", 3), ("cnt", 3),
    ("g1", 1), ("g2", 0), ("xa", 15), ("g2", 2), ("xa", 6), ("xa", 8), ("gb", 0), ("xa", 2), ("xs", 3),
    ("g2", 1), ("xa", 4), ("g1", 2), ("xs", 11), ("g2", 2), ("gb", 0), ("g2", 3), ("gb", 0), ("g1", 0),
    ("xs", 13), ("xa", 12), ("g1", 3), ("xa", 7), ("xa", 9), ("g2", 3), ("xs", 0), ("xa", 0), ("xa", 10),
    ("g1", 0), ("xa", 3), ("g1", 1), ("g1", 0), ("l1", 0), ("g2", 1), ("xs", 5), ("g2", 0), ("g1", 2),
    ("g1", 1), ("xa", 11), ("g2", 2), ("xs", 1), ("g1", 1), ("l1", 2), ("g2", 0), ("g1", 3), ("xa", 1),
    ("g1", 3), ("l1", 6), ("g2", 3), ("xa", 5), ("xa", 13), ("g1", 2), ("l1", 7), ("l1", 1), ("g2", 1),
    ("l1", 3), ("g2", 0), ("g1", 2), ("g2", 2), ("g1", 2), ("l1", 4), ("l1", 5), ("g2", 3), ("g2", 2),
    ("l2", 4), ("g2", 1), ("l2", 5), ("s2", 2), ("g2", 3), ("l2", 6), ("l2", 7), ("o2", 2), ("r2", 2),
    ("g2", 0), ("s2", 3), ("g2", 1), ("g2", 0), ("l2", 0), ("l2", 1), ("g2", 1), ("l2", 2), ("l2", 3),
    ("s2", 0), ("s2", 1), ("o2", 0), ("r2", 0), ("o2", 1), ("r2", 1), ("o2", 3), ("r2", 3), ("b2", 1),
    ("b2", 0), ("b2", 2), ("r2", 2), ("r2", 3), ("r2", 0), ("b2", 3), ("b1", 0), ("s1", 1), ("s1", 0),
    ("o1", 0), ("r1", 0), ("o1", 1), ("s1", 2), ("s1", 3), ("o1", 3), ("r2", 3), ("r2", 1), ("r2", 0),
    ("o1", 2), ("b1", 1), ("bs", 0), ("r1", 3), ("r2", 2), ("rb", 0), ("r2", 1), ("r1", 2), ("rb", 0),
    ("r1", 0), ("r1", 1), ("r1", 2), ("r1", 3), ("rb", 0), ("b1", 2), ("r2", 0), ("rb", 0), ("b1", 3),
    ("r1", 1), ("r1", 3), ("r1", 0), ("r2", 1), ("r2", 3), ("r1", 2), ("r1", 3), ("r1", 1), ("r2", 2),
    ("r1", 0), ("r1", 1), ("r1", 3), ("r2", 1), ("r2", 3), ("r1", 2), ("r2", 0), ("r2", 2), ("r1", 0),
    ("r1", 1), ("rb", 0), ("r1", 2),
)


def dot(a, b, dims):
    return lax.dot_general(a, b, dims, preferred_element_type=F32)


def gelu_and_slope(v):
    c = 0.7978845608
    square = v * v
    half = 0.5 + 0.5 * jnp.tanh(v * (c + (c * 0.044715) * square))
    value = v * half
    slope = half + (value - value * half) * (2.0 * c + (6.0 * c * 0.044715) * square)
    return value, slope


def kernel(
    sizes,
    x_in, near_in, edges_in, w_one_in, w_two_in, b_one_in, b_two_in, cot_in,
    out_ref, grad_in_ref, grad_one_ref, grad_two_ref, grad_bias_ref,
    w_one, w_two, rows_one, rows_two, slope_one, grad_two, terms, pair, got_one, got_two, relays,
    counts, scaling, near, biases, bias_sum, bias_terms, bias_pair, bias_got, bias_relay,
    send, recv, local, credit,
):
    Y, X, Z, r, width, cap, own = sizes
    planes, nf = Y * X, 2 * Y * X
    per = planes // TILES
    slots = own * cap
    cols_per = width // TILES
    rows_per = width // TILES
    f, z = lax.axis_index("feat"), lax.axis_index("grp")
    c = lax.rem(f, 2)
    x = lax.rem(lax.div(f, 2), X)
    y = lax.div(f, 2 * X)
    place = {"y": y, "x": x, "c": c, "z": z}
    extent = {"y": Y, "x": X, "z": Z}
    taken = [0, 0]
    pending = []
    pending_two = []

    def device(**moved):
        at = {**place, **moved}
        return ((at["y"] * X + at["x"]) * 2 + at["c"], at["z"])

    def copy_to(src, dst, dev, arrival=None):
        taken[0] += 1
        if arrival is None:
            taken[1] += 1
            arrival = taken[1] - 1
        return pltpu.make_async_remote_copy(
            src, dst, send.at[taken[0] - 1], recv.at[arrival], device_id=dev, device_id_type=MESH
        )

    def launch(copy, when=None, log=pending):
        if when is None:
            copy.start()
        else:
            pl.when(when)(copy.start)
        log.append((copy, when))

    def settle(copies):
        for copy, when in copies:
            if when is None:
                copy.wait_send()
            else:
                pl.when(when)(copy.wait_send)

    def arrived(copy, when=None):
        if when is None:
            copy.wait_recv()
        else:
            pl.when(when)(copy.wait_recv)

    def box(ref, cols, full, **moved):
        at = {**place, **moved}
        lead = [slice(None) if a in full else pl.ds(at[a], 1) for a in ("y", "x", "c", "z")]
        return ref.at[(*lead, slice(None), cols)]

    ends = jnp.logical_or(z == 0, z == Z - 1)
    inner = jnp.logical_not(ends)

    def flip(coordinate, bit):
        return coordinate + bit - 2 * bit * lax.rem(lax.div(coordinate, bit), 2)

    def around(axis, hop):
        return lax.rem(place[axis] + hop, extent[axis])

    def gather(ref, cols, first, order, log=pending):
        full = set()
        for stage, axis in enumerate(order):
            src = box(ref, cols, full)
            if stage == 0 and first is not None:
                src = first.at[(slice(None),) * 5 + (cols,)]
            copies = []
            if axis == "z":
                far = flip(z, 2)
                to_far = copy_to(src, box(ref, cols, full), device(z=far))
                to_near = copy_to(src, box(ref, cols, full), device(z=flip(z, 1)))
                to_end = copy_to(src, box(ref, cols, full), device(z=Z - 1 - z))
                handed = taken[1] - 1
                launch(to_far, None, log)
                launch(to_near, None, log)
                launch(to_end, inner, log)
                yield
                arrived(to_far)
                moved = box(ref, cols, full, z=far)
                launch(copy_to(moved, moved, device(z=flip(z, 1)), handed), inner, log)
                yield
                arrived(to_near)
                arrived(to_end)
            else:
                for hop in range(1, extent[axis]):
                    dev = device(**{axis: around(axis, hop)})
                    copies.append(copy_to(src, box(ref, cols, full), dev))
                    launch(copies[-1], None, log)
                yield
                for copy in copies:
                    arrived(copy)
            full.add(axis)
        whole = box(ref, cols, full)
        copy = copy_to(whole, whole, device(c=1 - c))
        launch(copy, None, log)
        yield
        arrived(copy)

    def reduce(ref, got, cols, order, result, relay):
        full = {"x", "y", "z"}

        def total(boxes, extra=None):
            value = box(ref, cols, full)[...].astype(F32)
            for part in boxes:
                value = value + part[...].astype(F32)
            return value

        def here(target, **moved):
            at = {"y": y, "x": x, "c": 0 * c, "z": z, **moved}
            lead = [slice(None) if a in full else pl.ds(at[a], 1) for a in ("y", "x", "c", "z")]
            return target.at[(*lead, slice(None), cols)]

        for stage, axis in enumerate(order):
            last = stage == len(order) - 1
            full.discard(axis)
            parts = []
            if axis == "z":
                near_z, far_z, end_z = flip(z, 1), flip(z, 2), Z - 1 - z
                to_near = copy_to(box(ref, cols, full, z=near_z), here(got), device(z=near_z))
                to_far = copy_to(box(ref, cols, full, z=far_z), here(got), device(z=far_z))
                to_end = copy_to(box(ref, cols, full, z=end_z), here(got), device(z=end_z))
                lead = [slice(None) if a in full else pl.ds(place[a], 1) for a in ("y", "x")]
                handed = here(got, z=near_z)
                held = here(got)
                if not last:
                    handed = held = relay.at[(*lead, slice(None), slice(None), slice(None), slice(None))]
                via = copy_to(box(ref, cols, full, z=end_z), handed, device(z=near_z))
                launch(via, ends)
                launch(to_far, ends)
                launch(to_near)
                launch(to_end, inner)
                yield
                arrived(via, inner)

                @pl.when(inner)
                def _():
                    mine = box(ref, cols, full, z=far_z)
                    mine[...] = (mine[...].astype(F32) + held[...].astype(F32)).astype(mine.dtype)

                launch(to_far, inner)
                yield
                arrived(to_near)
                arrived(to_far)
                arrived(to_end, inner)
                value = total([here(got, z=near_z), here(got, z=far_z)])
                if last:
                    result(value, cols)

                    @pl.when(inner)
                    def _():
                        result(here(got, z=end_z)[...].astype(F32), cols, True)
                else:
                    mine = box(ref, cols, full)
                    more = here(got, z=end_z)[...].astype(F32)
                    mine[...] = (value + jnp.where(inner, more, 0.0)).astype(mine.dtype)
            else:
                for hop in range(1, extent[axis]):
                    target = around(axis, hop)
                    copy = copy_to(
                        box(ref, cols, full, **{axis: target}), here(got), device(**{axis: target})
                    )
                    launch(copy)
                    parts.append((copy, here(got, **{axis: around(axis, extent[axis] - hop)})))
                yield
                for copy, _ in parts:
                    arrived(copy)
                value = total([part for _, part in parts])
                if last:
                    result(value, cols)
                else:
                    mine = box(ref, cols, full)
                    mine[...] = value.astype(mine.dtype)

    def finish(*parts):
        for part in parts:
            for _ in part:
                pass

    def rows_of(w, q):
        if per < X:
            lead = (pl.ds(lax.div(q * per, X), 1), pl.ds(lax.rem(q * per, X), per))
        else:
            lead = (pl.ds(q * (per // X), per // X), slice(None))
        return w.at[(*lead, slice(None), slice(None), slice(None), slice(None))]

    def act_rows(ref, q):
        return ref.at[pl.ds(q * per, per)]

    def tile_cols(u):
        if isinstance(u, int):
            return slice(u * cap, (u + 1) * cap)
        return pl.ds(pl.multiple_of(u * cap, cap), cap)

    def each_cluster(work):
        def one(u, carry):
            work(u)
            return carry

        lax.fori_loop(0, own, one, 0)

    barrier = pltpu.get_barrier_semaphore()
    for hop in range(1, nf):
        pl.semaphore_signal(barrier, 1, device_id=(lax.rem(f + hop, nf), z), device_id_type=MESH)
    for hop in range(1, Z):
        pl.semaphore_signal(barrier, 1, device_id=(f, lax.rem(z + hop, Z)), device_id_type=MESH)

    every = slice(0, 128)
    parts = [slice(q * cols_per, (q + 1) * cols_per) for q in range(TILES)]
    near_copy = pltpu.make_async_copy(near_in.at[pl.ds(f * own, own)], near, local.at[0])
    w_one_copy = pltpu.make_async_copy(w_one_in, box(w_one, slice(None), ()), local.at[1])
    w_two_copy = pltpu.make_async_copy(w_two_in, box(w_two, slice(None), ()), local.at[2])
    x_copy = pltpu.make_async_copy(
        x_in.at[:, pl.ds(pl.multiple_of(f * slots, slots), slots)],
        rows_one.at[lax.div(f, 2), c],
        local.at[3],
    )
    cot_copy = pltpu.make_async_copy(cot_in, grad_two, local.at[4])
    near_copy.start()
    w_one_copy.start()
    w_two_copy.start()
    x_copy.start()
    shape = (r, r)
    same = lax.broadcasted_iota(jnp.int32, shape, 0) == lax.broadcasted_iota(jnp.int32, shape, 1)
    lane = lax.broadcasted_iota(jnp.int32, (r, 128), 1)
    block = jnp.zeros((r, 128), F32)
    for layer, ref in enumerate((b_one_in, b_two_in)):
        column = jnp.sum(jnp.where(same, ref[...].astype(F32), 0.0), axis=1, keepdims=True)
        block = jnp.where(lane == layer, column, block)
    box(biases, every, ())[...] = block.astype(BF).reshape(1, 1, 1, 1, r, 128)

    pl.semaphore_wait(barrier, nf - 1 + Z - 1)

    work = {}
    for q, cols in enumerate(parts):
        work["g1", q] = gather(w_one, cols, w_one_in, GATHER_ONE[q])
        work["g2", q] = gather(w_two, cols, w_two_in, GATHER_TWO[q], pending_two)
    work["gb", 0] = gather(biases, every, None, "xyz")

    turns = [(dy, dx, dc) for dc in range(2) for dy in range(Y) for dx in range(X)][1:]
    turns.sort(key=lambda turn: (turn[0] > 0) + (turn[1] > 0))
    groups = [turns[i * len(turns) // 7 : (i + 1) * len(turns) // 7] for i in range(7)]
    x_copies = {}

    seen = set()

    def once(name):
        first = name not in seen
        seen.add(name)
        return first

    def send_x(i, u):
        for dy, dx, dc in groups[i]:
            dev = device(y=lax.rem(y + dy, Y), x=lax.rem(x + dx, X), c=lax.rem(c + dc, 2))
            mine = x_in.at[:, pl.ds(pl.multiple_of(dev[0] * slots + u * cap, cap), cap)]
            there = rows_one.at[lax.div(f, 2), c, :, u * cap : (u + 1) * cap]
            x_copies[dy, dx, dc, u] = copy_to(mine, there, dev)
            launch(x_copies[dy, dx, dc, u])

    strip = min(64, cap)
    strips = cap // strip

    def count(i):
        u, part = i * own // 4, i % (4 // own)
        if i == 0:
            near_copy.wait()
            bias_sum[...] = jnp.zeros_like(bias_sum)
        edges = edges_in[pl.ds(f * own + u, 1), :]
        total_edges = edges.astype(F32)
        near_u = near.at[u]
        scaling[u] = jnp.where(edges > 0, 1.0 / (total_edges + 1.0), 0.0)

        def strip_counts(i, carry):
            start = pl.multiple_of(i * strip, strip)
            slot = start + lax.broadcasted_iota(jnp.int32, (strip, cap), 0)
            other = lax.broadcasted_iota(jnp.int32, (strip, cap), 1)
            acc = jnp.where(slot == other, 2.0, 0.0)
            for k in range(near.shape[1]):
                target = jnp.where(k < edges, near_u[k : k + 1, :], -1)
                acc = acc + jnp.where(slot == target, 1.0, 0.0)
            counts[u, pl.ds(start, strip), :] = acc.astype(BF)
            return carry

        share = strips * own // 4
        lax.fori_loop(part * share, (part + 1) * share, strip_counts, 0)

    def aggregate(value, u):
        return (scaling[u] * dot(value, counts[u], NN)).astype(BF)

    def aggregate_back(value, u):
        normed = (scaling[u] * value.astype(BF).astype(F32)).astype(BF)
        return dot(normed, counts[u], NT)

    def first_rows(owner, u):
        ref = rows_one.at[lax.div(owner, 2), lax.rem(owner, 2), :, u * cap : (u + 1) * cap]
        ref[...] = aggregate(ref[...], u)

    def rows_from(i, u):
        if i == 7:
            if once("x"):
                x_copy.wait()
            first_rows(f, u)
            return
        for dy, dx, dc in groups[i]:
            arrived(x_copies[dy, dx, dc, u])
            owner = device(
                y=lax.rem(y + Y - dy, Y), x=lax.rem(x + X - dx, X), c=lax.rem(c + dc, 2)
            )
            first_rows(owner[0], u)

    def linear(w, rows, layer, q, u):
        weight = w[..., parts[q]].reshape(width, cols_per)
        a = rows[:, :, :, tile_cols(u)].reshape(width, cap)
        bias = rows_of(biases, q)[...].reshape(rows_per, 128)[:, layer : layer + 1]
        return dot(weight, a, TN) + bias.astype(F32)

    tile = (per, 2, Z * r, cap)

    def layer_one(q, u):
        value, slope = gelu_and_slope(linear(w_one, rows_one, 0, q, u))
        act_rows(slope_one, q)[:, :, :, tile_cols(u)] = slope.astype(BF).reshape(tile)
        rows = aggregate(value.astype(BF), u)
        act_rows(rows_two, q)[:, :, :, tile_cols(u)] = rows.reshape(tile)

    def add_bias(q, u, value):
        ref = bias_sum.at[pl.ds(q * rows_per, rows_per), :]
        folded = sum(value[:, i * 128 : (i + 1) * 128] for i in range(cap // 128))
        ref[...] = ref[...] + folded

    out_copies = []

    def layer_two(q, u):
        if once("cot"):
            cot_copy.wait()
        value, slope = gelu_and_slope(linear(w_two, rows_two, 1, q, u))
        ref = rows_of(terms, q).at[..., tile_cols(u)]
        ref[...] = value.astype(BF).reshape(ref.shape)
        ref = act_rows(grad_two, q).at[:, :, :, tile_cols(u)]
        grad = (ref[...].astype(F32).reshape(rows_per, cap) * slope).astype(BF)
        ref[...] = grad.reshape(tile)
        add_bias(q, u, grad.astype(F32))
        if u < own - 1:
            return
        copy = pltpu.make_async_copy(
            rows_of(terms, q).at[..., pl.ds(0, slots)], rows_of(out_ref, q), local.at[5 + q]
        )
        copy.start()
        out_copies.append(copy)

    lanes = lax.broadcasted_iota(jnp.int32, (width, 128), 1)

    def bias_of_two():
        total = jnp.where(lanes == 1, jnp.sum(bias_sum[...], axis=1, keepdims=True), 0.0)
        bias_terms[...] = total.astype(BF).reshape(bias_terms.shape)
        bias_sum[...] = jnp.zeros_like(bias_sum)

    def pair_half(rows, grads, core, q):
        a = rows[:, pl.ds(core, 1)].reshape(width // 2, slots)
        b = act_rows(grads, q)[...].reshape(rows_per, slots)
        return dot(a, b, NT).reshape(Y, X, 1, Z, r, cols_per)

    def pair_send(target, q, value):
        half = target.at[:, :, pl.ds(1 - c, 1), :, :, parts[q]]
        half[...] = value.astype(BF)
        copy = copy_to(half, pair.at[..., parts[q]], device(c=1 - c))
        launch(copy)
        return copy

    def pair_add(target, q, value, copy):
        arrived(copy)
        half = target.at[:, :, pl.ds(c, 1), :, :, parts[q]]
        half[...] = (value + pair[..., parts[q]].astype(F32)).astype(BF)

    def owner_result(ref):
        def result(value, cols, add=False):
            value = value.reshape(r, value.shape[-1])
            ref[:, cols] = ref[:, cols] + value if add else value

        return result

    layers = {
        "1": (rows_one, rows_two, w_two, got_one, REDUCE_ONE, grad_one_ref),
        "2": (rows_two, grad_two, terms, got_two, REDUCE_TWO, grad_two_ref),
    }
    relayed = 0
    for name, (_, _, target, got, orders, out) in layers.items():
        for q in range(TILES):
            relay = None
            if orders[q][0] == "z":
                relay = relays.at[..., relayed * cols_per : (relayed + 1) * cols_per]
                relayed += 1
            work["r" + name, q] = reduce(target, got, parts[q], orders[q], owner_result(out), relay)
    work["rb", 0] = reduce(
        bias_terms, bias_got, every, "zyx", owner_result(grad_bias_ref), bias_relay
    )
    pair_copies = {}
    def sibling_half(name, q):
        if name == "2":
            if q * cols_per < slots and once("out"):
                for copy in out_copies:
                    copy.wait()
        elif once("s1"):
            settle(pending_two)
            pl.semaphore_wait(credit, 1)
        rows, grads, target = layers[name][:3]
        pair_copies[name, q] = pair_send(target, q, pair_half(rows, grads, 1 - c, q))

    def own_half(name, q):
        rows, grads, target = layers[name][:3]
        pair_add(target, q, pair_half(rows, grads, c, q), pair_copies[name, q])
        if name == "2":
            seen.add(("pair", q))
            if all(("pair", i) in seen for i in range(TILES)):
                pl.semaphore_signal(credit, 1, device_id=device(c=1 - c), device_id_type=MESH)

    def back_two(q):
        if once("b2"):
            bias_of_two()

        def work(u):
            weight = rows_of(w_two, q)[...].reshape(rows_per, width)
            grad = dot(weight, grad_two[:, :, :, tile_cols(u)].reshape(width, cap), NN)
            hidden = aggregate_back(grad, u).astype(BF).astype(F32)
            slope = act_rows(slope_one, q)[:, :, :, tile_cols(u)].reshape(rows_per, cap).astype(F32)
            grad = (hidden * slope).astype(BF)
            act_rows(rows_two, q)[:, :, :, tile_cols(u)] = grad.reshape(tile)
            add_bias(q, u, grad.astype(F32))

        each_cluster(work)

    grad_one = rows_two
    def bias_send():
        total = jnp.sum(bias_sum[...], axis=1, keepdims=True)
        both = jnp.where(lanes == 0, total, bias_terms[...].reshape(width, 128).astype(F32))
        bias_terms[...] = both.astype(BF).reshape(bias_terms.shape)
        copy = copy_to(bias_terms.at[:, :, pl.ds(1 - c, 1)], bias_pair, device(c=1 - c))
        launch(copy)
        pair_copies["b"] = copy

    def bias_add():
        arrived(pair_copies["b"])
        mine = bias_terms.at[:, :, pl.ds(c, 1)]
        mine[...] = (mine[...].astype(F32) + bias_pair[...].astype(F32)).astype(BF)

    grad_in = grad_two
    grad_place = grad_in_ref.at[:, pl.ds(pl.multiple_of(f * slots, slots), slots)]

    def back_one(i):
        k = (3, 1, 2, 0)[i]
        if per == 1:
            q = lax.rem(y + k // 2, Y) * X + lax.rem(x + k % 2, X)
        else:
            q = lax.rem(y + k, Y)

        def work(u):
            weight = rows_of(w_one, q)[...].reshape(rows_per, width)
            grad = dot(weight, grad_one[:, :, :, tile_cols(u)].reshape(width, cap), NN)
            value = aggregate_back(grad, u).astype(BF)
            act_rows(grad_in, q)[:, :, :, tile_cols(u)] = value.reshape(tile)

        each_cluster(work)
        for j in range(2 * per):
            to = q * (2 * per) + j
            hop = lax.rem(to + nf - f, nf)
            taken[0] += 1
            copy = pltpu.make_async_remote_copy(
                grad_in.at[lax.div(to, 2), lax.rem(to, 2)], grad_place,
                send.at[taken[0] - 1], recv.at[recv.shape[0] - nf + hop],
                device_id=(to, z), device_id_type=MESH,
            )
            launch(copy, None if k else to != f)

    calls = {
        "xs": send_x, "xa": rows_from, "cnt": count, "l1": layer_one, "l2": layer_two,
        "s1": functools.partial(sibling_half, "1"), "o1": functools.partial(own_half, "1"),
        "s2": functools.partial(sibling_half, "2"), "o2": functools.partial(own_half, "2"),
        "b2": back_two, "b1": back_one,
    }
    places = {}
    for name, q in ORDER:
        if name in ("xs", "xa", "l1", "l2"):
            calls[name](q // own, q % own)
        elif name in calls:
            calls[name](q)
        elif name == "bs":
            bias_send()
        else:
            stage = places[name, q] = places.get((name, q), -1) + 1
            if stage == 0 and name == "rb":
                bias_add()
            if stage == 1 and name[0] == "g" and once("shards"):
                w_one_copy.wait()
                w_two_copy.wait()
                cot_copy.start()
            next(work[name, q], None)
            if stage == 5:
                finish(work[name, q])
    finish(*work.values())
    own_copy = pltpu.make_async_copy(grad_in.at[lax.div(f, 2), c], grad_place, local.at[0])
    own_copy.start()
    for hop in range(1, nf):
        sender = lax.rem(f + nf - hop, nf)
        pltpu.make_async_remote_copy(
            grad_in.at[0, 0], grad_in_ref.at[:, pl.ds(pl.multiple_of(sender * slots, slots), slots)],
            send.at[0], recv.at[recv.shape[0] - nf + hop],
            device_id=(f, z), device_id_type=MESH,
        ).wait_recv()
    own_copy.wait()
    settle(pending)


def body(mesh, features, neighbours, edge_counts, w_one, b_one, w_two, b_two, cotangent):
    nf, Z = mesh.shape["feat"], mesh.shape["grp"]
    side = 1
    while side * side * 2 < nf:
        side *= 2
    Y = X = side
    r, width = w_one.shape
    clusters, cap = edge_counts.shape
    own = clusters // nf
    slots = own * cap
    planes = Y * X
    group = features.shape[0]
    shard = (1, 1, 1, 1, r, width)
    act = (planes, 2, group, slots)
    table = (Y, X, 2, Z, r, width)
    half = (Y, X, 1, Z, r, width)
    anywhere = pl.BlockSpec(memory_space=pl.ANY)
    vmem = pl.BlockSpec(memory_space=pltpu.VMEM)
    scratch = [pltpu.VMEM(table, BF)] * 2
    scratch += [pltpu.VMEM(act, BF)] * 4
    scratch += [pltpu.VMEM(table, BF)] + [pltpu.VMEM(half, BF)] * 3
    relayed = sum(order[0] == "z" for order in REDUCE_ONE + REDUCE_TWO)
    scratch += [pltpu.VMEM((Y, X, 1, 1, r, max(1, relayed) * (width // TILES)), BF)]
    scratch += [
        pltpu.VMEM((own, cap, cap), BF),
        pltpu.VMEM((own, 1, cap), F32),
        pltpu.VMEM((own, *neighbours.shape[1:]), jnp.int32),
        pltpu.VMEM((Y, X, 2, Z, r, 128), BF),
        pltpu.VMEM((width, 128), F32),
        pltpu.VMEM((Y, X, 2, Z, r, 128), BF),
        pltpu.VMEM((Y, X, 1, Z, r, 128), BF),
        pltpu.VMEM((Y, X, 1, Z, r, 128), BF),
        pltpu.VMEM((Y, X, 1, 1, r, 128), BF),
        pltpu.SemaphoreType.DMA((256,)),
        pltpu.SemaphoreType.DMA((256,)),
        pltpu.SemaphoreType.DMA((16,)),
        pltpu.SemaphoreType.REGULAR,
    ]
    out, grad_in, grad_one, grad_two, grad_bias = pl.pallas_call(
        functools.partial(kernel, (Y, X, Z, r, width, cap, own)),
        out_shape=(
            jax.ShapeDtypeStruct((Y, X, 2, Z, r, slots), BF),
            jax.ShapeDtypeStruct((group, nf * slots), BF),
            jax.ShapeDtypeStruct((r, width), F32),
            jax.ShapeDtypeStruct((r, width), F32),
            jax.ShapeDtypeStruct((r, 128), F32),
        ),
        in_specs=[anywhere, anywhere, vmem, anywhere, anywhere, vmem, vmem, anywhere],
        out_specs=(anywhere, anywhere, vmem, vmem, vmem),
        scratch_shapes=scratch,
        compiler_params=pltpu.CompilerParams(
            collective_id=0, has_side_effects=True, vmem_limit_bytes=67_000_000
        ),
    )(
        features,
        neighbours,
        edge_counts,
        w_one.reshape(shard),
        w_two.reshape(shard),
        b_one.reshape(1, r),
        b_two.reshape(1, r),
        cotangent.reshape(act),
    )
    return (
        out.reshape(width, slots),
        grad_in.astype(F32),
        grad_one,
        grad_bias[:, 0],
        grad_two,
        grad_bias[:, 1],
    )


def solution(mesh):
    both = ("feat", "grp")
    in_specs = (
        P("feat", "grp"),
        P("grp", None, None),
        P("grp", None),
        P(both, None),
        P(both),
        P(both, None),
        P(both),
        P(None, ("grp", "feat")),
    )
    out_specs = (
        P(None, ("grp", "feat")),
        P("feat", "grp"),
        P(both, None),
        P(both),
        P(both, None),
        P(both),
    )
    return jax.shard_map(
        functools.partial(body, mesh), mesh=mesh, in_specs=in_specs, out_specs=out_specs, check_vma=False
    )
```

```python
import functools

import jax
import jax.numpy as jnp
from jax import lax
from jax.experimental import pallas as pl
from jax.experimental.pallas import tpu as pltpu
from jax.sharding import PartitionSpec as P

BF, F32 = jnp.bfloat16, jnp.float32
MESH = pl.DeviceIdType.MESH
TILES = 4
NN = (((1,), (0,)), ((), ()))
NT = (((1,), (1,)), ((), ()))
TN = (((0,), (0,)), ((), ()))
GATHER_ONE = ("xyz", "yxz", "xyz", "zyx")
GATHER_TWO = ("zyx", "yxz", "zyx", "zxy")
REDUCE_TWO = ("xyz", "yxz", "zxy", "zyx")
REDUCE_ONE = ("zxy", "yxz", "zxy", "yxz")
ORDER = (
    ("gb", 0), ("g1", 1), ("g1", 0), ("g1", 3), ("xs", 6), ("g2", 3), ("cnt", 0), ("g1", 0), ("gb", 0),
    ("xs", 12), ("g1", 1), ("cnt", 1), ("xs", 2), ("g1", 2), ("g2", 2), ("xs", 8), ("xs", 4), ("g1", 3),
    ("xs", 10), ("cnt", 2), ("gb", 0), ("g1", 0), ("xs", 7), ("xs", 9), ("xa", 14), ("g1", 3), ("cnt", 3),
    ("g1", 1), ("g2", 0), ("xa", 15), ("g2", 2), ("xa", 8), ("gb", 0), ("xa", 2), ("xs", 3), ("g2", 1),
    ("xa", 4), ("g1", 2), ("xs", 11), ("g2", 2), ("gb", 0), ("g2", 3), ("gb", 0), ("g1", 0), ("xs", 13),
    ("xa", 12), ("g1", 3), ("xa", 6), ("xa", 7), ("xa", 9), ("g2", 3), ("xs", 0), ("xa", 10), ("g1", 0),
    ("xa", 3), ("g1", 1), ("xa", 0), ("g1", 0), ("l1", 0), ("g2", 1), ("xs", 5), ("g2", 0), ("g1", 2),
    ("g1", 1), ("xa", 11), ("g2", 2), ("xs", 1), ("g1", 1), ("l1", 2), ("g2", 0), ("g1", 3), ("xa", 1),
    ("g1", 3), ("l1", 6), ("g2", 3), ("xa", 5), ("xa", 13), ("g1", 2), ("l1", 7), ("l1", 1), ("g2", 1),
    ("l1", 3), ("g2", 0), ("g1", 2), ("g2", 2), ("g1", 2), ("l1", 4), ("l1", 5), ("g2", 3), ("g2", 2),
    ("l2", 4), ("g2", 1), ("l2", 5), ("s2", 2), ("g2", 3), ("l2", 6), ("l2", 7), ("o2", 2), ("r2", 2),
    ("g2", 0), ("g2", 1), ("s2", 3), ("g2", 0), ("l2", 0), ("l2", 1), ("g2", 1), ("l2", 2), ("l2", 3),
    ("s2", 0), ("s2", 1), ("o2", 0), ("r2", 0), ("o2", 3), ("o2", 1), ("r2", 1), ("r2", 3), ("b2", 1),
    ("b2", 0), ("b2", 2), ("r2", 2), ("r2", 3), ("r2", 0), ("b2", 3), ("b1", 0), ("s1", 1), ("s1", 0),
    ("o1", 0), ("r1", 0), ("o1", 1), ("s1", 2), ("s1", 3), ("o1", 3), ("r2", 3), ("r2", 1), ("r2", 0),
    ("o1", 2), ("b1", 1), ("bs", 0), ("r1", 3), ("r2", 2), ("rb", 0), ("r2", 1), ("r1", 2), ("rb", 0),
    ("r1", 0), ("r1", 1), ("r1", 2), ("r1", 3), ("rb", 0), ("b1", 2), ("r2", 0), ("rb", 0), ("b1", 3),
    ("r1", 1), ("r1", 3), ("r1", 0), ("r2", 1), ("r2", 3), ("r1", 2), ("r1", 3), ("r1", 1), ("r2", 2),
    ("r1", 0), ("r1", 1), ("r1", 3), ("r2", 1), ("r2", 3), ("r1", 2), ("r2", 0), ("r2", 2), ("r1", 0),
    ("r1", 1), ("rb", 0), ("r1", 2),
)


def dot(a, b, dims):
    return lax.dot_general(a, b, dims, preferred_element_type=F32)


def gelu_and_slope(v):
    c = 0.7978845608
    square = v * v
    half = 0.5 + 0.5 * jnp.tanh(v * (c + (c * 0.044715) * square))
    value = v * half
    slope = half + (value - value * half) * (2.0 * c + (6.0 * c * 0.044715) * square)
    return value, slope


def kernel(
    sizes,
    x_in, near_in, edges_in, w_one_in, w_two_in, b_one_in, b_two_in, cot_in,
    out_ref, grad_in_ref, grad_one_ref, grad_two_ref, grad_bias_ref,
    w_one, w_two, rows_one, rows_two, slope_one, grad_two, terms, pair, got_one, got_two, relays, out_held,
    counts, scaling, near, biases, bias_sum, bias_terms, bias_pair, bias_got, bias_relay,
    send, recv, local, credit,
):
    Y, X, Z, r, width, cap, own = sizes
    planes, nf = Y * X, 2 * Y * X
    per = planes // TILES
    slots = own * cap
    cols_per = width // TILES
    rows_per = width // TILES
    f, z = lax.axis_index("feat"), lax.axis_index("grp")
    c = lax.rem(f, 2)
    x = lax.rem(lax.div(f, 2), X)
    y = lax.div(f, 2 * X)
    place = {"y": y, "x": x, "c": c, "z": z}
    extent = {"y": Y, "x": X, "z": Z}
    taken = [0, 0]
    pending = []
    pending_two = []

    def device(**moved):
        at = {**place, **moved}
        return ((at["y"] * X + at["x"]) * 2 + at["c"], at["z"])

    def copy_to(src, dst, dev, arrival=None):
        taken[0] += 1
        if arrival is None:
            taken[1] += 1
            arrival = taken[1] - 1
        return pltpu.make_async_remote_copy(
            src, dst, send.at[taken[0] - 1], recv.at[arrival], device_id=dev, device_id_type=MESH
        )

    def launch(copy, when=None, log=pending):
        if when is None:
            copy.start()
        else:
            pl.when(when)(copy.start)
        log.append((copy, when))

    def settle(copies):
        for copy, when in copies:
            if when is None:
                copy.wait_send()
            else:
                pl.when(when)(copy.wait_send)

    def arrived(copy, when=None):
        if when is None:
            copy.wait_recv()
        else:
            pl.when(when)(copy.wait_recv)

    def box(ref, cols, full, **moved):
        at = {**place, **moved}
        lead = [slice(None) if a in full else pl.ds(at[a], 1) for a in ("y", "x", "c", "z")]
        return ref.at[(*lead, slice(None), cols)]

    ends = jnp.logical_or(z == 0, z == Z - 1)
    inner = jnp.logical_not(ends)

    def flip(coordinate, bit):
        return coordinate + bit - 2 * bit * lax.rem(lax.div(coordinate, bit), 2)

    def around(axis, hop):
        return lax.rem(place[axis] + hop, extent[axis])

    def gather(ref, cols, first, order, log=pending):
        full = set()
        for stage, axis in enumerate(order):
            src = box(ref, cols, full)
            if stage == 0 and first is not None:
                src = first.at[(slice(None),) * 5 + (cols,)]
            copies = []
            if axis == "z":
                far = flip(z, 2)
                to_far = copy_to(src, box(ref, cols, full), device(z=far))
                to_near = copy_to(src, box(ref, cols, full), device(z=flip(z, 1)))
                to_end = copy_to(src, box(ref, cols, full), device(z=Z - 1 - z))
                handed = taken[1] - 1
                launch(to_far, None, log)
                launch(to_near, None, log)
                launch(to_end, inner, log)
                yield
                arrived(to_far)
                moved = box(ref, cols, full, z=far)
                launch(copy_to(moved, moved, device(z=flip(z, 1)), handed), inner, log)
                yield
                arrived(to_near)
                arrived(to_end)
            else:
                for hop in range(1, extent[axis]):
                    dev = device(**{axis: around(axis, hop)})
                    copies.append(copy_to(src, box(ref, cols, full), dev))
                    launch(copies[-1], None, log)
                yield
                for copy in copies:
                    arrived(copy)
            full.add(axis)
        whole = box(ref, cols, full)
        copy = copy_to(whole, whole, device(c=1 - c))
        launch(copy, None, log)
        yield
        arrived(copy)

    def reduce(ref, got, cols, order, result, relay):
        full = {"x", "y", "z"}

        def total(boxes, extra=None):
            value = box(ref, cols, full)[...].astype(F32)
            for part in boxes:
                value = value + part[...].astype(F32)
            return value

        def here(target, **moved):
            at = {"y": y, "x": x, "c": 0 * c, "z": z, **moved}
            lead = [slice(None) if a in full else pl.ds(at[a], 1) for a in ("y", "x", "c", "z")]
            return target.at[(*lead, slice(None), cols)]

        for stage, axis in enumerate(order):
            last = stage == len(order) - 1
            full.discard(axis)
            parts = []
            if axis == "z":
                near_z, far_z, end_z = flip(z, 1), flip(z, 2), Z - 1 - z
                to_near = copy_to(box(ref, cols, full, z=near_z), here(got), device(z=near_z))
                to_far = copy_to(box(ref, cols, full, z=far_z), here(got), device(z=far_z))
                to_end = copy_to(box(ref, cols, full, z=end_z), here(got), device(z=end_z))
                lead = [slice(None) if a in full else pl.ds(place[a], 1) for a in ("y", "x")]
                handed = here(got, z=near_z)
                held = here(got)
                if not last:
                    handed = held = relay.at[(*lead, slice(None), slice(None), slice(None), slice(None))]
                via = copy_to(box(ref, cols, full, z=end_z), handed, device(z=near_z))
                launch(via, ends)
                launch(to_far, ends)
                launch(to_near)
                launch(to_end, inner)
                yield
                arrived(via, inner)

                @pl.when(inner)
                def _():
                    mine = box(ref, cols, full, z=far_z)
                    mine[...] = (mine[...].astype(F32) + held[...].astype(F32)).astype(mine.dtype)

                launch(to_far, inner)
                yield
                arrived(to_near)
                arrived(to_far)
                arrived(to_end, inner)
                value = total([here(got, z=near_z), here(got, z=far_z)])
                if last:
                    result(value, cols)

                    @pl.when(inner)
                    def _():
                        result(here(got, z=end_z)[...].astype(F32), cols, True)
                else:
                    mine = box(ref, cols, full)
                    more = here(got, z=end_z)[...].astype(F32)
                    mine[...] = (value + jnp.where(inner, more, 0.0)).astype(mine.dtype)
            else:
                for hop in range(1, extent[axis]):
                    target = around(axis, hop)
                    copy = copy_to(
                        box(ref, cols, full, **{axis: target}), here(got), device(**{axis: target})
                    )
                    launch(copy)
                    parts.append((copy, here(got, **{axis: around(axis, extent[axis] - hop)})))
                yield
                for copy, _ in parts:
                    arrived(copy)
                value = total([part for _, part in parts])
                if last:
                    result(value, cols)
                else:
                    mine = box(ref, cols, full)
                    mine[...] = value.astype(mine.dtype)

    def finish(*parts):
        for part in parts:
            for _ in part:
                pass

    def rows_of(w, q):
        if per < X:
            lead = (pl.ds(lax.div(q * per, X), 1), pl.ds(lax.rem(q * per, X), per))
        else:
            lead = (pl.ds(q * (per // X), per // X), slice(None))
        return w.at[(*lead, slice(None), slice(None), slice(None), slice(None))]

    def act_rows(ref, q):
        return ref.at[pl.ds(q * per, per)]

    def tile_cols(u):
        if isinstance(u, int):
            return slice(u * cap, (u + 1) * cap)
        return pl.ds(pl.multiple_of(u * cap, cap), cap)

    def each_cluster(work):
        def one(u, carry):
            work(u)
            return carry

        lax.fori_loop(0, own, one, 0)

    barrier = pltpu.get_barrier_semaphore()
    for hop in range(1, nf):
        pl.semaphore_signal(barrier, 1, device_id=(lax.rem(f + hop, nf), z), device_id_type=MESH)
    for hop in range(1, Z):
        pl.semaphore_signal(barrier, 1, device_id=(f, lax.rem(z + hop, Z)), device_id_type=MESH)

    every = slice(0, 128)
    parts = [slice(q * cols_per, (q + 1) * cols_per) for q in range(TILES)]
    near_copy = pltpu.make_async_copy(near_in.at[pl.ds(f * own, own)], near, local.at[0])
    w_one_copy = pltpu.make_async_copy(w_one_in, box(w_one, slice(None), ()), local.at[1])
    w_two_copy = pltpu.make_async_copy(w_two_in, box(w_two, slice(None), ()), local.at[2])
    x_copy = pltpu.make_async_copy(
        x_in.at[:, pl.ds(pl.multiple_of(f * slots, slots), slots)],
        rows_one.at[lax.div(f, 2), c],
        local.at[3],
    )
    cot_copy = pltpu.make_async_copy(cot_in, grad_two, local.at[4])
    near_copy.start()
    w_one_copy.start()
    w_two_copy.start()
    x_copy.start()
    shape = (r, r)
    same = lax.broadcasted_iota(jnp.int32, shape, 0) == lax.broadcasted_iota(jnp.int32, shape, 1)
    lane = lax.broadcasted_iota(jnp.int32, (r, 128), 1)
    block = jnp.zeros((r, 128), F32)
    for layer, ref in enumerate((b_one_in, b_two_in)):
        column = jnp.sum(jnp.where(same, ref[...].astype(F32), 0.0), axis=1, keepdims=True)
        block = jnp.where(lane == layer, column, block)
    box(biases, every, ())[...] = block.astype(BF).reshape(1, 1, 1, 1, r, 128)

    pl.semaphore_wait(barrier, nf - 1 + Z - 1)

    work = {}
    for q, cols in enumerate(parts):
        work["g1", q] = gather(w_one, cols, w_one_in, GATHER_ONE[q])
        work["g2", q] = gather(w_two, cols, w_two_in, GATHER_TWO[q], pending_two)
    work["gb", 0] = gather(biases, every, None, "xyz")

    turns = [(dy, dx, dc) for dc in range(2) for dy in range(Y) for dx in range(X)][1:]
    turns.sort(key=lambda turn: (turn[0] > 0) + (turn[1] > 0))
    groups = [turns[i * len(turns) // 7 : (i + 1) * len(turns) // 7] for i in range(7)]
    x_copies = {}

    seen = set()

    def once(name):
        first = name not in seen
        seen.add(name)
        return first

    def send_x(i, u):
        for dy, dx, dc in groups[i]:
            dev = device(y=lax.rem(y + dy, Y), x=lax.rem(x + dx, X), c=lax.rem(c + dc, 2))
            mine = x_in.at[:, pl.ds(pl.multiple_of(dev[0] * slots + u * cap, cap), cap)]
            there = rows_one.at[lax.div(f, 2), c, :, u * cap : (u + 1) * cap]
            x_copies[dy, dx, dc, u] = copy_to(mine, there, dev)
            launch(x_copies[dy, dx, dc, u])

    strip = min(64, cap)
    strips = cap // strip

    def count(i):
        u, part = i * own // 4, i % (4 // own)
        if i == 0:
            near_copy.wait()
            bias_sum[...] = jnp.zeros_like(bias_sum)
        edges = edges_in[pl.ds(f * own + u, 1), :]
        total_edges = edges.astype(F32)
        near_u = near.at[u]
        scaling[u] = jnp.where(edges > 0, 1.0 / (total_edges + 1.0), 0.0)

        def strip_counts(i, carry):
            start = pl.multiple_of(i * strip, strip)
            slot = start + lax.broadcasted_iota(jnp.int32, (strip, cap), 0)
            other = lax.broadcasted_iota(jnp.int32, (strip, cap), 1)
            acc = jnp.where(slot == other, 2.0, 0.0)
            for k in range(near.shape[1]):
                target = jnp.where(k < edges, near_u[k : k + 1, :], -1)
                acc = acc + jnp.where(slot == target, 1.0, 0.0)
            counts[u, pl.ds(start, strip), :] = acc.astype(BF)
            return carry

        share = strips * own // 4
        lax.fori_loop(part * share, (part + 1) * share, strip_counts, 0)

    def aggregate(value, u):
        return (scaling[u] * dot(value, counts[u], NN)).astype(BF)

    def aggregate_back(value, u):
        normed = (scaling[u] * value.astype(BF).astype(F32)).astype(BF)
        return dot(normed, counts[u], NT)

    def first_rows(owner, u):
        ref = rows_one.at[lax.div(owner, 2), lax.rem(owner, 2), :, u * cap : (u + 1) * cap]
        ref[...] = aggregate(ref[...], u)

    def rows_from(i, u):
        if i == 7:
            if once("x"):
                x_copy.wait()
            first_rows(f, u)
            return
        for dy, dx, dc in groups[i]:
            arrived(x_copies[dy, dx, dc, u])
            owner = device(
                y=lax.rem(y + Y - dy, Y), x=lax.rem(x + X - dx, X), c=lax.rem(c + dc, 2)
            )
            first_rows(owner[0], u)

    def linear(w, rows, layer, q, u):
        weight = w[..., parts[q]].reshape(width, cols_per)
        a = rows[:, :, :, tile_cols(u)].reshape(width, cap)
        bias = rows_of(biases, q)[...].reshape(rows_per, 128)[:, layer : layer + 1]
        return dot(weight, a, TN) + bias.astype(F32)

    tile = (per, 2, Z * r, cap)

    def layer_one(q, u):
        value, slope = gelu_and_slope(linear(w_one, rows_one, 0, q, u))
        act_rows(slope_one, q)[:, :, :, tile_cols(u)] = slope.astype(BF).reshape(tile)
        rows = aggregate(value.astype(BF), u)
        act_rows(rows_two, q)[:, :, :, tile_cols(u)] = rows.reshape(tile)

    def add_bias(q, u, value):
        ref = bias_sum.at[pl.ds(q * rows_per, rows_per), :]
        folded = sum(value[:, i * 128 : (i + 1) * 128] for i in range(cap // 128))
        ref[...] = ref[...] + folded

    out_copies = []

    def layer_two(q, u):
        if once("cot"):
            cot_copy.wait()
        value, slope = gelu_and_slope(linear(w_two, rows_two, 1, q, u))
        if u == 0 and out_copies:
            out_copies[-1].wait()
        ref = out_held.at[..., tile_cols(u)]
        ref[...] = value.astype(BF).reshape(ref.shape)
        ref = act_rows(grad_two, q).at[:, :, :, tile_cols(u)]
        grad = (ref[...].astype(F32).reshape(rows_per, cap) * slope).astype(BF)
        ref[...] = grad.reshape(tile)
        add_bias(q, u, grad.astype(F32))
        if u < own - 1:
            return
        copy = pltpu.make_async_copy(out_held, rows_of(out_ref, q), local.at[5 + q])
        copy.start()
        out_copies.append(copy)

    lanes = lax.broadcasted_iota(jnp.int32, (width, 128), 1)

    def bias_of_two():
        total = jnp.where(lanes == 1, jnp.sum(bias_sum[...], axis=1, keepdims=True), 0.0)
        bias_terms[...] = total.astype(BF).reshape(bias_terms.shape)
        bias_sum[...] = jnp.zeros_like(bias_sum)

    def pair_half(rows, grads, core, q):
        a = rows[:, pl.ds(core, 1)].reshape(width // 2, slots)
        b = act_rows(grads, q)[...].reshape(rows_per, slots)
        return dot(a, b, NT).reshape(Y, X, 1, Z, r, cols_per)

    def pair_send(target, q, value):
        half = target.at[:, :, pl.ds(1 - c, 1), :, :, parts[q]]
        half[...] = value.astype(BF)
        copy = copy_to(half, pair.at[..., parts[q]], device(c=1 - c))
        launch(copy)
        return copy

    def pair_add(target, q, value, copy):
        arrived(copy)
        half = target.at[:, :, pl.ds(c, 1), :, :, parts[q]]
        half[...] = (value + pair[..., parts[q]].astype(F32)).astype(BF)

    def owner_result(ref):
        def result(value, cols, add=False):
            value = value.reshape(r, value.shape[-1])
            ref[:, cols] = ref[:, cols] + value if add else value

        return result

    layers = {
        "1": (rows_one, rows_two, w_two, got_one, REDUCE_ONE, grad_one_ref),
        "2": (rows_two, grad_two, terms, got_two, REDUCE_TWO, grad_two_ref),
    }
    relayed = 0
    for name, (_, _, target, got, orders, out) in layers.items():
        for q in range(TILES):
            relay = None
            if orders[q][0] == "z":
                relay = relays.at[..., relayed * cols_per : (relayed + 1) * cols_per]
                relayed += 1
            work["r" + name, q] = reduce(target, got, parts[q], orders[q], owner_result(out), relay)
    work["rb", 0] = reduce(
        bias_terms, bias_got, every, "zyx", owner_result(grad_bias_ref), bias_relay
    )
    pair_copies = {}
    def sibling_half(name, q):
        if name == "1" and once("s1"):
            settle(pending_two)
            pl.semaphore_wait(credit, 1)
        rows, grads, target = layers[name][:3]
        pair_copies[name, q] = pair_send(target, q, pair_half(rows, grads, 1 - c, q))

    def own_half(name, q):
        rows, grads, target = layers[name][:3]
        pair_add(target, q, pair_half(rows, grads, c, q), pair_copies[name, q])
        if name == "2":
            seen.add(("pair", q))
            if all(("pair", i) in seen for i in range(TILES)):
                pl.semaphore_signal(credit, 1, device_id=device(c=1 - c), device_id_type=MESH)

    def back_two(q):
        if once("b2"):
            bias_of_two()

        def work(u):
            weight = rows_of(w_two, q)[...].reshape(rows_per, width)
            grad = dot(weight, grad_two[:, :, :, tile_cols(u)].reshape(width, cap), NN)
            hidden = aggregate_back(grad, u).astype(BF).astype(F32)
            slope = act_rows(slope_one, q)[:, :, :, tile_cols(u)].reshape(rows_per, cap).astype(F32)
            grad = (hidden * slope).astype(BF)
            act_rows(rows_two, q)[:, :, :, tile_cols(u)] = grad.reshape(tile)
            add_bias(q, u, grad.astype(F32))

        each_cluster(work)

    grad_one = rows_two
    def bias_send():
        total = jnp.sum(bias_sum[...], axis=1, keepdims=True)
        both = jnp.where(lanes == 0, total, bias_terms[...].reshape(width, 128).astype(F32))
        bias_terms[...] = both.astype(BF).reshape(bias_terms.shape)
        copy = copy_to(bias_terms.at[:, :, pl.ds(1 - c, 1)], bias_pair, device(c=1 - c))
        launch(copy)
        pair_copies["b"] = copy

    def bias_add():
        arrived(pair_copies["b"])
        mine = bias_terms.at[:, :, pl.ds(c, 1)]
        mine[...] = (mine[...].astype(F32) + bias_pair[...].astype(F32)).astype(BF)

    grad_in = grad_two
    grad_place = grad_in_ref.at[:, pl.ds(pl.multiple_of(f * slots, slots), slots)]

    def back_one(i):
        k = (3, 1, 2, 0)[i]
        if per == 1:
            q = lax.rem(y + k // 2, Y) * X + lax.rem(x + k % 2, X)
        else:
            q = lax.rem(y + k, Y)

        def work(u):
            weight = rows_of(w_one, q)[...].reshape(rows_per, width)
            grad = dot(weight, grad_one[:, :, :, tile_cols(u)].reshape(width, cap), NN)
            value = aggregate_back(grad, u).astype(BF)
            act_rows(grad_in, q)[:, :, :, tile_cols(u)] = value.reshape(tile)

        each_cluster(work)
        for j in range(2 * per):
            to = q * (2 * per) + j
            hop = lax.rem(to + nf - f, nf)
            taken[0] += 1
            copy = pltpu.make_async_remote_copy(
                grad_in.at[lax.div(to, 2), lax.rem(to, 2)], grad_place,
                send.at[taken[0] - 1], recv.at[recv.shape[0] - nf + hop],
                device_id=(to, z), device_id_type=MESH,
            )
            launch(copy, None if k else to != f)

    calls = {
        "xs": send_x, "xa": rows_from, "cnt": count, "l1": layer_one, "l2": layer_two,
        "s1": functools.partial(sibling_half, "1"), "o1": functools.partial(own_half, "1"),
        "s2": functools.partial(sibling_half, "2"), "o2": functools.partial(own_half, "2"),
        "b2": back_two, "b1": back_one,
    }
    places = {}
    for name, q in ORDER:
        if name in ("xs", "xa", "l1", "l2"):
            calls[name](q // own, q % own)
        elif name in calls:
            calls[name](q)
        elif name == "bs":
            bias_send()
        else:
            stage = places[name, q] = places.get((name, q), -1) + 1
            if stage == 0 and name == "rb":
                bias_add()
            if stage == 1 and name[0] == "g" and once("shards"):
                w_one_copy.wait()
                w_two_copy.wait()
                cot_copy.start()
            next(work[name, q], None)
            if stage == 5:
                finish(work[name, q])
    finish(*work.values())
    own_copy = pltpu.make_async_copy(grad_in.at[lax.div(f, 2), c], grad_place, local.at[0])
    own_copy.start()
    for hop in range(1, nf):
        sender = lax.rem(f + nf - hop, nf)
        pltpu.make_async_remote_copy(
            grad_in.at[0, 0], grad_in_ref.at[:, pl.ds(pl.multiple_of(sender * slots, slots), slots)],
            send.at[0], recv.at[recv.shape[0] - nf + hop],
            device_id=(f, z), device_id_type=MESH,
        ).wait_recv()
    own_copy.wait()
    out_copies[-1].wait()
    settle(pending)


def body(mesh, features, neighbours, edge_counts, w_one, b_one, w_two, b_two, cotangent):
    nf, Z = mesh.shape["feat"], mesh.shape["grp"]
    side = 1
    while side * side * 2 < nf:
        side *= 2
    Y = X = side
    r, width = w_one.shape
    clusters, cap = edge_counts.shape
    own = clusters // nf
    slots = own * cap
    planes = Y * X
    group = features.shape[0]
    shard = (1, 1, 1, 1, r, width)
    act = (planes, 2, group, slots)
    table = (Y, X, 2, Z, r, width)
    half = (Y, X, 1, Z, r, width)
    anywhere = pl.BlockSpec(memory_space=pl.ANY)
    vmem = pl.BlockSpec(memory_space=pltpu.VMEM)
    scratch = [pltpu.VMEM(table, BF)] * 2
    scratch += [pltpu.VMEM(act, BF)] * 4
    scratch += [pltpu.VMEM(table, BF)] + [pltpu.VMEM(half, BF)] * 3
    relayed = sum(order[0] == "z" for order in REDUCE_ONE + REDUCE_TWO)
    scratch += [pltpu.VMEM((Y, X, 1, 1, r, max(1, relayed) * (width // TILES)), BF)]
    per = planes // TILES
    lead = (1, per) if per < X else (per // X, X)
    scratch += [pltpu.VMEM((*lead, 2, Z, r, slots), BF)]
    scratch += [
        pltpu.VMEM((own, cap, cap), BF),
        pltpu.VMEM((own, 1, cap), F32),
        pltpu.VMEM((own, *neighbours.shape[1:]), jnp.int32),
        pltpu.VMEM((Y, X, 2, Z, r, 128), BF),
        pltpu.VMEM((width, 128), F32),
        pltpu.VMEM((Y, X, 2, Z, r, 128), BF),
        pltpu.VMEM((Y, X, 1, Z, r, 128), BF),
        pltpu.VMEM((Y, X, 1, Z, r, 128), BF),
        pltpu.VMEM((Y, X, 1, 1, r, 128), BF),
        pltpu.SemaphoreType.DMA((256,)),
        pltpu.SemaphoreType.DMA((256,)),
        pltpu.SemaphoreType.DMA((16,)),
        pltpu.SemaphoreType.REGULAR,
    ]
    out, grad_in, grad_one, grad_two, grad_bias = pl.pallas_call(
        functools.partial(kernel, (Y, X, Z, r, width, cap, own)),
        out_shape=(
            jax.ShapeDtypeStruct((Y, X, 2, Z, r, slots), BF),
            jax.ShapeDtypeStruct((group, nf * slots), BF),
            jax.ShapeDtypeStruct((r, width), F32),
            jax.ShapeDtypeStruct((r, width), F32),
            jax.ShapeDtypeStruct((r, 128), F32),
        ),
        in_specs=[anywhere, anywhere, vmem, anywhere, anywhere, vmem, vmem, anywhere],
        out_specs=(anywhere, anywhere, vmem, vmem, vmem),
        scratch_shapes=scratch,
        compiler_params=pltpu.CompilerParams(
            collective_id=0, has_side_effects=True, vmem_limit_bytes=67_000_000
        ),
    )(
        features,
        neighbours,
        edge_counts,
        w_one.reshape(shard),
        w_two.reshape(shard),
        b_one.reshape(1, r),
        b_two.reshape(1, r),
        cotangent.reshape(act),
    )
    return (
        out.reshape(width, slots),
        grad_in.astype(F32),
        grad_one,
        grad_bias[:, 0],
        grad_two,
        grad_bias[:, 1],
    )


def solution(mesh):
    both = ("feat", "grp")
    in_specs = (
        P("feat", "grp"),
        P("grp", None, None),
        P("grp", None),
        P(both, None),
        P(both),
        P(both, None),
        P(both),
        P(None, ("grp", "feat")),
    )
    out_specs = (
        P(None, ("grp", "feat")),
        P("feat", "grp"),
        P(both, None),
        P(both),
        P(both, None),
        P(both),
    )
    return jax.shard_map(
        functools.partial(body, mesh), mesh=mesh, in_specs=in_specs, out_specs=out_specs, check_vma=False
    )
```
